256 devices in a mesh: row: 16 (over x, y), col: 16 (over z, core).
Axes of the slice: x: 4, y: 4, z: 8, core: 2. Of those that a mesh axis runs over, the one named last changes fastest.
Arguments:
- covariance: float32 [4, 16, 256, 4, 16, 256], P(None, 'row', None, None, 'col'), as said below
Outputs:
- factored: float32 [4, 16, 256, 4, 16, 256], P(None, 'row', None, None, 'col')
Inputs may be any that keep to these rules, and one draw needn't show every extreme that they name: covariance is symmetric and positive definite, its smallest eigenvalue at least a hundredth of its largest diagonal entry.
All inputs are finite; a program needn't handle non-finite values.
Results may differ from the reference program's by a relative error of at most 0.0019.
Values may be sent and summed in bfloat16 or wider, within the bound.
A program may use at most 128 MiB of HBM per device.

```python
import jax
import jax.numpy as jnp
from jax import lax

M = 16384
NB = 256
PANELS = 2
LBR = 4
LBC = 4
N_ROW = 16
N_COL = 16


def draw_covariance(key, part):
    key = jax.random.fold_in(key, 7)
    key_loadings, key_ridge = jax.random.split(key, 2)
    factor_count = M // 16
    loadings = jax.random.randint(key_loadings, (M, factor_count), -2, 3).astype(jnp.float32)
    weight = 1.0 / (2.0 * factor_count)
    coupled = jnp.dot(loadings, loadings.T, precision=lax.Precision.HIGHEST) * weight
    ridge_terms = 0.25 + 0.75 * jax.random.uniform(key_ridge, (M,), jnp.float32)
    positions = jnp.arange(M)
    matrix = coupled.at[positions, positions].add(ridge_terms)
    return matrix.reshape(LBR, N_ROW, NB, LBC, N_COL, NB)


def setup_inputs(seed: int = 0) -> dict:
    arg_keys = jax.random.split(jax.random.key(seed), 2)
    return {
        "covariance": draw_covariance(jax.random.fold_in(arg_keys[1], 71), 0),
    }


def reference(covariance):
    matrix = covariance.reshape(M, M)
    for panel in range(PANELS):
        start = panel * NB
        stop = start + NB
        factor = jnp.linalg.cholesky(matrix[start:stop, start:stop])
        solved = lax.linalg.triangular_solve(factor, matrix[stop:, start:stop], left_side=False, lower=True, transpose_a=True)
        matrix = matrix.at[start:stop, start:stop].set(factor)
        matrix = matrix.at[stop:, start:stop].set(solved)
        rounded = lax.optimization_barrier(solved.astype(jnp.bfloat16)).astype(jnp.float32)
        update = jnp.dot(rounded, rounded.T, precision=lax.Precision.HIGHEST)
        matrix = matrix.at[stop:, stop:].set(matrix[stop:, stop:] - update)
    return matrix.reshape(LBR, N_ROW, NB, LBC, N_COL, NB)
```

```python
import jax
import jax.numpy as jnp
from jax import lax
from jax.experimental import pallas as pl
from jax.experimental.pallas import tpu as pltpu
from jax.sharding import PartitionSpec as P

MESH = pl.DeviceIdType.MESH
HI = lax.Precision.HIGHEST
F32 = jnp.float32
BF16 = jnp.bfloat16
NB = 256
PARTS = 8


def lane_pick(value, lane):
    return jnp.take_along_axis(value, jnp.full(value.shape, lane, jnp.int32), axis=1)


def small_inverse(v_ref, half):
    group = lax.broadcasted_iota(jnp.int32, (8, 8, 128), 0)
    sub = lax.broadcasted_iota(jnp.int32, (8, 128), 0)

    def panel(p, _):
        r = v_ref[p]
        base = 8 * p + half
        s, low, t, inv = {}, {}, {}, []
        for k in range(8):
            c = lane_pick(r, base + k)
            for i in range(k, 8):
                s[i, k] = jnp.broadcast_to(c[i : i + 1], (8, 128))
        for k in range(8):
            rk = lax.rsqrt(s[k, k])
            inv.append(rk)
            for i in range(k + 1, 8):
                low[i, k] = s[i, k] * rk
            for j in range(k + 1, 8):
                for i in range(j, 8):
                    s[i, j] = s[i, j] - low[i, k] * low[j, k]
        for i in range(8):
            t[i, i] = inv[i]
            for j in range(i):
                acc = low[i, j] * t[j, j]
                for m in range(j + 1, i):
                    acc = acc + low[i, m] * t[m, j]
                t[i, j] = -(inv[i] * acc)
        rows = [jnp.broadcast_to(r[j : j + 1], (8, 128)) for j in range(8)]
        new = []
        for k in range(8):
            acc = t[k, 0] * rows[0]
            for j in range(1, k + 1):
                acc = acc + t[k, j] * rows[j]
            new.append(acc)
        out = new[0]
        for k in range(1, 8):
            out = jnp.where(sub == k, new[k], out)
        update = None
        for j in range(8):
            z = t[7, j] * new[7]
            for k in range(j, 7):
                z = z + t[k, j] * new[k]
            c = jnp.stack([lane_pick(v_ref[g], base + j) for g in range(8)])
            term = c * z[None]
            update = term if update is None else update + term
        v = v_ref[...]
        v_ref[...] = jnp.where(group > p, v - update, jnp.where(group == p, out[None], v))
        return 0

    lax.fori_loop(0, 8, panel, 0)


def factor(g_ref, v_ref, ready, after):
    lane = lax.broadcasted_iota(jnp.int32, (64, 128), 1)
    row = lax.broadcasted_iota(jnp.int32, (64, 128), 0)
    lanes = lax.broadcasted_iota(jnp.int32, (64, NB), 1)

    def block(q, _):
        half = lax.rem(q, 2) * 64
        rows = pl.ds(pl.multiple_of(64 * q, 64), 64)
        tile = pl.ds(pl.multiple_of((q // 2) * 128, 128), 128)
        mine = (lane >= half) & (lane < half + 64)
        eye = ((lane - (64 - half)) == row).astype(F32)
        v_ref[...] = jnp.where(mine, g_ref[rows, tile], eye).reshape(8, 8, 128)
        small_inverse(v_ref, half)
        ready(q)
        t = jnp.where(mine, 0.0, v_ref[...].reshape(64, 128))
        gq = g_ref[rows, :]
        u = jnp.dot(t, jnp.concatenate([gq, gq], axis=0), precision=HI, preferred_element_type=F32)
        g_ref[rows, :] = u
        after(q, rows, u)
        left = jnp.where(lanes >= 64 * (q + 1), u[:, :NB], 0.0)
        g_ref[...] -= lax.dot_general(
            left, u, (((0,), (0,)), ((), ())), precision=HI, preferred_element_type=F32
        )
        return 0

    lax.fori_loop(0, 4, block, 0)


def every(*conditions):
    result = conditions[0]
    for condition in conditions[1:]:
        result = result & condition
    return result


def gather_kernel(
    a_ref, w0row, w1row, w0col, w1col, newcol,
    rraw, craw, linv, w10, low1, a01, a11, g0, g1, v_ref, r1, c1,
    load_sem, r_send, r_recv, c_send, c_recv, l_send, l_recv, w_send, w_recv, x_send, x_recv,
):
    row, col = lax.axis_index("row"), lax.axis_index("col")
    x, y, z, k = row // 4, row % 4, col // 2, col % 2

    def device(x, y, z, k):
        return ((x + 4) % 4 * 4 + (y + 4) % 4, (z + 8) % 8 * 2 + (k + 2) % 2)

    def shifted(offset, sign=1):
        dx, dy, dz, dk = offset
        return (
            (x + sign * dx + 4) % 4, (y + sign * dy + 4) % 4,
            (z + sign * dz + 8) % 8, (k + sign * dk + 2) % 2,
        )

    r_edges = [
        ((0, 0, 1, 0), lambda x, y, z, k: z <= 3),
        ((0, 0, -1, 0), lambda x, y, z, k: (z == 0) | (z >= 6)),
        ((0, 0, 0, 1), lambda x, y, z, k: z >= 0),
    ]
    c_edges = [
        [
            ((1, 0, 0, 0), lambda x, y, z, k: (y == 0) & (x <= 1)),
            ((-1, 0, 0, 0), lambda x, y, z, k: (y == 0) & (x == 0)),
            ((0, 1, 0, 0), lambda x, y, z, k: y == 0),
            ((0, -1, 0, 0), lambda x, y, z, k: (y == 0) | (y == 3)),
        ],
        [
            ((1, 0, 0, 0), lambda x, y, z, k: (y == 1) & (x <= 1)),
            ((-1, 0, 0, 0), lambda x, y, z, k: (y == 1) & (x == 0)),
            ((0, -1, 0, 0), lambda x, y, z, k: y == 1),
            ((0, 1, 0, 0), lambda x, y, z, k: (y == 1) | (y == 2)),
        ],
    ]

    def trunk(x, y, k):
        return every(x == 0, y == 0, k == 1)

    l_edges = [
        ((0, 0, 1, 0), lambda x, y, z, k: trunk(x, y, k) & ((z == 0) | (z == 2))),
        ((0, 0, 2, 0), lambda x, y, z, k: trunk(x, y, k) & ((z == 0) | (z == 2))),
        ((0, 0, -1, 0), lambda x, y, z, k: trunk(x, y, k) & ((z == 0) | (z == 6))),
        ((0, 0, -2, 0), lambda x, y, z, k: trunk(x, y, k) & (z == 0)),
        ((0, 0, 0, 1), lambda x, y, z, k: jnp.where((x + y + z) == 0, k == 0, k == 1)),
    ]
    corner = every(row == 0, col == 0)
    beside = every(row == 0, col == 1)
    below = every(row == 1, col == 1)
    on_trunk = trunk(x, y, k)
    r_source = z == 0
    c_source = [every(x == 0, y == 0), every(x == 0, y == 1)]

    def r_load(t):
        return pltpu.make_async_copy(
            a_ref.at[:, t, :], rraw.at[k, :, pl.ds(128 * t, 128)], load_sem.at[t]
        )

    def c_load(s, t):
        return pltpu.make_async_copy(
            a_ref.at[pl.ds(0, NB), t, :], craw.at[s, :, pl.ds(128 * t, 128)], load_sem.at[2 + t]
        )

    @pl.when(r_source)
    def _():
        for t in range(2):
            r_load(t).start()

    for s in range(2):
        @pl.when(c_source[s])
        def _():
            for t in range(8):
                c_load(s, t).start()

    barrier = pltpu.get_barrier_semaphore()

    def greet(target):
        pl.semaphore_signal(barrier, inc=1, device_id=device(*target), device_id_type=MESH)

    awaited = jnp.int32(0)
    for offset, sends in r_edges + c_edges[0] + c_edges[1] + l_edges:
        awaited = awaited + sends(x, y, z, k).astype(jnp.int32)
        parent = shifted(offset, -1)

        @pl.when(sends(*parent))
        def _():
            greet(parent)

    awaited = awaited + jnp.where(on_trunk, 15, 0) + jnp.where(beside, 1, 0)
    awaited = awaited + jnp.where(below, 1, 0) + jnp.where(corner, 1, 0)

    @pl.when((row != 0) & (k == 1))
    def _():
        greet((0, 0, z, 1))

    @pl.when(corner)
    def _():
        greet((0, 0, 0, 1))
        greet((0, 1, 0, 1))

    @pl.when(below)
    def _():
        greet((0, 0, 0, 0))

    pl.semaphore_wait(barrier, awaited)

    def remote(src, dst, send, recv, target):
        return pltpu.make_async_remote_copy(
            src_ref=src, dst_ref=dst, send_sem=send, recv_sem=recv,
            device_id=device(*target), device_id_type=MESH,
        )

    def r_copy(n, s, e):
        part = rraw.at[s, pl.ds(pl.multiple_of(n * (1024 // PARTS), 1024 // PARTS), 1024 // PARTS), :]
        return remote(part, part, r_send.at[e, n], r_recv.at[s, n], shifted(r_edges[e][0]))

    def c_copy(n, s, e):
        part = craw.at[s, pl.ds(pl.multiple_of(n * (NB // PARTS), NB // PARTS), NB // PARTS), :]
        return remote(part, part, c_send.at[s, e, n], c_recv.at[s, n], shifted(c_edges[s][e][0]))

    def l_part(p, q):
        return linv.at[p, pl.ds(pl.multiple_of(64 * q, 64), 64), :]

    def l_copy(p, q, e):
        return remote(
            l_part(p, q), l_part(p, q), l_send.at[p, q, e], l_recv.at[p, q], shifted(l_edges[e][0])
        )

    def l_spread(p, q, t):
        return remote(
            l_part(p, q), l_part(p, q), l_send.at[p, q, 4 + t], l_recv.at[p, q], (t // 4, t % 4, z, 1)
        )

    def w_copy(e):
        return remote(w10, w10, w_send.at[e], w_recv, shifted(l_edges[e][0]))

    def w_spread(t):
        return remote(w10, w10, w_send.at[4 + t], w_recv, (t // 4, t % 4, z, 1))

    def a01_copy():
        return remote(craw.at[0, :, pl.ds(0, NB)], a01, x_send.at[0], x_recv.at[0], (0, 0, 0, 0))

    def a11_copy():
        return remote(craw.at[1, :, pl.ds(0, NB)], a11, x_send.at[1], x_recv.at[1], (0, 0, 0, 0))

    def low1_copy():
        return remote(low1, low1, x_send.at[2], x_recv.at[2], (0, 1, 0, 1))

    for s in range(2):
        @pl.when(c_source[s])
        def _():
            for t in range(8):
                c_load(s, t).wait()

    @pl.when(beside)
    def _():
        a01_copy().start()

    @pl.when(below)
    def _():
        a11_copy().start()

    @pl.when(r_source)
    def _():
        for t in range(2):
            r_load(t).wait()

    def send_r(n):
        for e, (offset, sends) in enumerate(r_edges):
            @pl.when(sends(x, y, z, k))
            def _():
                r_copy(n, k, e).start()

    def send_c(n, s):
        for e, (offset, sends) in enumerate(c_edges[s]):
            @pl.when(sends(x, y, z, k))
            def _():
                c_copy(n, s, e).start()

    def from_source(n, _):
        @pl.when(r_source)
        def _():
            send_r(n)

        for s in range(2):
            @pl.when(c_source[s])
            def _():
                send_c(n, s)

        return 0

    lax.fori_loop(0, PARTS, from_source, 0)

    @pl.when(corner)
    def _():
        eye = (
            lax.broadcasted_iota(jnp.int32, (NB, NB), 0) == lax.broadcasted_iota(jnp.int32, (NB, NB), 1)
        ).astype(F32)
        g0[:, :NB] = craw[0, :, :NB]
        g0[:, 2 * NB :] = eye
        g1[:, NB:] = eye

        def ready0(q):
            @pl.when(q == 0)
            def _():
                a01_copy().wait_recv()
                g0[:, NB : 2 * NB] = a01[...]
                a11_copy().wait_recv()
                g1[:, :NB] = a11[...]

        def after0(q, rows, u):
            linv[0, rows, :] = u[:, 2 * NB :]
            l_copy(0, q, 4).start()
            w = u[:, NB : 2 * NB].astype(BF16)
            w10[rows, :] = w
            g1[:, :NB] -= lax.dot_general(w, w, (((0,), (0,)), ((), ())), preferred_element_type=F32)

        factor(g0, v_ref, ready0, after0)
        w_copy(4).start()

        def after1(q, rows, u):
            linv[1, rows, :] = u[:, NB:]
            l_copy(1, q, 4).start()
            low1[rows, :] = u[:, :NB]

        factor(g1, v_ref, lambda q: None, after1)
        low1_copy().start()

    def forward(n, _):
        @pl.when(jnp.logical_not(r_source))
        def _():
            r_copy(n, k, 0).wait_recv()
            send_r(n)

        for s in range(2):
            @pl.when(jnp.logical_not(c_source[s]))
            def _():
                c_copy(n, s, 0).wait_recv()
                send_c(n, s)

        return 0

    lax.fori_loop(0, PARTS, forward, 0)

    def other(n, _):
        r_copy(n, 1 - k, 0).wait_recv()
        return 0

    def pass_on(p):
        def piece(q, _):
            @pl.when(jnp.logical_not(corner))
            def _():
                l_copy(p, q, 0).wait_recv()
                for e, (offset, sends) in enumerate(l_edges):
                    @pl.when(sends(x, y, z, k))
                    def _():
                        l_copy(p, q, e).start()

            @pl.when(on_trunk)
            def _():
                def spread(t, _):
                    l_spread(p, q, t).start()
                    return 0

                lax.fori_loop(1, 16, spread, 0)

            return 0

        lax.fori_loop(0, 4, piece, 0)

    pass_on(0)

    @pl.when(jnp.logical_not(corner))
    def _():
        w_copy(0).wait_recv()
        for e, (offset, sends) in enumerate(l_edges):
            @pl.when(sends(x, y, z, k))
            def _():
                w_copy(e).start()

    @pl.when(on_trunk)
    def _():
        def spread(t, _):
            w_spread(t).start()
            return 0

        lax.fori_loop(1, 16, spread, 0)

    lax.fori_loop(0, PARTS, other, 0)

    upper = lax.broadcasted_iota(jnp.int32, (NB, NB), 1) > lax.broadcasted_iota(jnp.int32, (NB, NB), 0)
    nt = (((1,), (1,)), ((), ()))
    tn = (((0,), (0,)), ((), ()))
    for b in range(4):
        rows = pl.ds(NB * b, NB)
        solved = lax.dot_general(rraw[0, rows, :], linv[0], nt, precision=HI, preferred_element_type=F32)
        newcol[rows, :] = solved
        rounded = solved.astype(BF16)
        if b == 0:
            rounded = jnp.where(row == 0, jnp.zeros_like(rounded), rounded)
        w0row[rows, :] = rounded
        r1[rows, :] = rraw[1, rows, :] - jnp.dot(rounded, w10[...], preferred_element_type=F32)
        solved = jnp.dot(linv[0], craw[0, :, rows], precision=HI, preferred_element_type=F32)
        rounded = solved.astype(BF16)
        if b == 0:
            rounded = jnp.where(col == 0, jnp.zeros_like(rounded), rounded)
        w0col[:, rows] = rounded
        c1[:, rows] = craw[1, :, rows] - lax.dot_general(w10[...], rounded, tn, preferred_element_type=F32)

    pass_on(1)

    for b in range(4):
        rows = pl.ds(NB * b, NB)
        solved = lax.dot_general(r1[rows, :], linv[1], nt, precision=HI, preferred_element_type=F32)
        rounded = solved.astype(BF16)
        if b == 0:
            rounded = jnp.where(row <= 1, jnp.zeros_like(rounded), rounded)
            solved = jnp.where(row == 0, r1[rows, :], solved)
        w1row[rows, :] = rounded

        @pl.when(col == 1)
        def _():
            newcol[rows, :] = solved

        solved = jnp.dot(linv[1], c1[:, rows], precision=HI, preferred_element_type=F32)
        rounded = solved.astype(BF16)
        if b == 0:
            rounded = jnp.where(col <= 1, jnp.zeros_like(rounded), rounded)
        w1col[:, rows] = rounded

    @pl.when(corner)
    def _():
        newcol[pl.ds(0, NB), :] = jnp.where(upper, 0.0, g0[:, :NB].T)

    @pl.when(below)
    def _():
        low1_copy().wait_recv()
        newcol[pl.ds(0, NB), :] = jnp.where(upper, 0.0, low1[...].T)

    def drain(n, _):
        for e, (offset, sends) in enumerate(r_edges):
            @pl.when(sends(x, y, z, k))
            def _():
                r_copy(n, k, e).wait_send()

        for s in range(2):
            for e, (offset, sends) in enumerate(c_edges[s]):
                @pl.when(sends(x, y, z, k))
                def _():
                    c_copy(n, s, e).wait_send()

        return 0

    lax.fori_loop(0, PARTS, drain, 0)
    for e, (offset, sends) in enumerate(l_edges):
        @pl.when(sends(x, y, z, k))
        def _():
            w_copy(e).wait_send()
            for p in range(2):
                for q in range(4):
                    l_copy(p, q, e).wait_send()

    @pl.when(on_trunk)
    def _():
        def spread(t, _):
            w_spread(t).wait_send()
            for p in range(2):
                for q in range(4):
                    l_spread(p, q, t).wait_send()
            return 0

        lax.fori_loop(1, 16, spread, 0)

    @pl.when(beside)
    def _():
        a01_copy().wait_send()

    @pl.when(below)
    def _():
        a11_copy().wait_send()

    @pl.when(corner)
    def _():
        low1_copy().wait_send()


def trailing_kernel(a_ref, w0row, w1row, w0col, w1col, newcol, o_ref):
    col = lax.axis_index("col")
    update = jnp.dot(w0row[...], w0col[...], preferred_element_type=F32)
    update += jnp.dot(w1row[...], w1col[...], preferred_element_type=F32)
    for t in range(8):
        part = a_ref[:, t, :] - update[:, 128 * t : 128 * (t + 1)]
        if t < 2:
            part = jnp.where(col <= 1, newcol[:, 128 * t : 128 * (t + 1)], part)
        o_ref[:, t, :] = part


def on_device(covariance):
    shape = covariance.shape
    a = covariance.reshape(1024, 8, 128)
    vmem = pl.BlockSpec(memory_space=pltpu.VMEM)
    dma = pltpu.SemaphoreType.DMA
    panels = pl.pallas_call(
        gather_kernel,
        out_shape=(
            jax.ShapeDtypeStruct((1024, NB), BF16),
            jax.ShapeDtypeStruct((1024, NB), BF16),
            jax.ShapeDtypeStruct((NB, 1024), BF16),
            jax.ShapeDtypeStruct((NB, 1024), BF16),
            jax.ShapeDtypeStruct((1024, NB), F32),
        ),
        in_specs=[pl.BlockSpec(memory_space=pl.ANY)],
        out_specs=(vmem,) * 5,
        scratch_shapes=[
            pltpu.VMEM((2, 1024, NB), F32),
            pltpu.VMEM((2, NB, 1024), F32),
            pltpu.VMEM((2, NB, NB), F32),
            pltpu.VMEM((NB, NB), BF16),
            pltpu.VMEM((NB, NB), F32),
            pltpu.VMEM((NB, NB), F32),
            pltpu.VMEM((NB, NB), F32),
            pltpu.VMEM((NB, 3 * NB), F32),
            pltpu.VMEM((NB, 2 * NB), F32),
            pltpu.VMEM((8, 8, 128), F32),
            pltpu.VMEM((1024, NB), F32),
            pltpu.VMEM((NB, 1024), F32),
            dma((10,)),
            dma((3, PARTS)),
            dma((2, PARTS)),
            dma((2, 4, PARTS)),
            dma((2, PARTS)),
            dma((2, 4, 20)),
            dma((2, 4)),
            dma((20,)),
            dma(()),
            dma((3,)),
            dma((3,)),
        ],
        compiler_params=pltpu.CompilerParams(
            collective_id=0, has_side_effects=True, vmem_limit_bytes=48 << 20
        ),
        name="panels",
    )(a)
    steps = 8
    rows = 1024 // steps
    out = pl.pallas_call(
        trailing_kernel,
        grid=(steps,),
        out_shape=jax.ShapeDtypeStruct((1024, 8, 128), F32),
        in_specs=[
            pl.BlockSpec((rows, 8, 128), lambda i: (i, 0, 0)),
            pl.BlockSpec((rows, NB), lambda i: (i, 0)),
            pl.BlockSpec((rows, NB), lambda i: (i, 0)),
            pl.BlockSpec((NB, 1024), lambda i: (0, 0)),
            pl.BlockSpec((NB, 1024), lambda i: (0, 0)),
            pl.BlockSpec((rows, NB), lambda i: (i, 0)),
        ],
        out_specs=pl.BlockSpec((rows, 8, 128), lambda i: (i, 0, 0)),
        compiler_params=pltpu.CompilerParams(vmem_limit_bytes=32 << 20),
        name="trailing",
    )(a, *panels)
    return out.reshape(shape)


def solution(mesh):
    spec = P(None, "row", None, None, "col", None)
    return jax.shard_map(
        on_device, mesh=mesh, in_specs=(spec,), out_specs=spec, check_vma=False
    )
```

```python
import jax
import jax.numpy as jnp
from jax import lax
from jax.experimental import pallas as pl
from jax.experimental.pallas import tpu as pltpu
from jax.sharding import PartitionSpec as P

MESH = pl.DeviceIdType.MESH
HI = lax.Precision.HIGHEST
F32 = jnp.float32
BF16 = jnp.bfloat16
NB = 256
R_PARTS = [(32, 0, 8, 0), (32, 256, 8, 0), (32, 512, 16, 8)]
C_PARTS = [(16, 0, 16, 0), (16, 256, 16, 0)]
PARTS = R_PARTS + C_PARTS + C_PARTS
HOP = 4


def lane_pick(value, lane):
    return jnp.take_along_axis(value, jnp.full(value.shape, lane, jnp.int32), axis=1)


def small_inverse(v_ref, half):
    group = lax.broadcasted_iota(jnp.int32, (8, 8, 128), 0)
    sub = lax.broadcasted_iota(jnp.int32, (8, 128), 0)

    def panel(p, _):
        r = v_ref[p]
        base = 8 * p + half
        s, low, t, inv = {}, {}, {}, []
        for k in range(8):
            c = lane_pick(r, base + k)
            for i in range(k, 8):
                s[i, k] = jnp.broadcast_to(c[i : i + 1], (8, 128))
        for k in range(8):
            rk = lax.rsqrt(s[k, k])
            inv.append(rk)
            for i in range(k + 1, 8):
                low[i, k] = s[i, k] * rk
            for j in range(k + 1, 8):
                for i in range(j, 8):
                    s[i, j] = s[i, j] - low[i, k] * low[j, k]
        for i in range(8):
            t[i, i] = inv[i]
            for j in range(i):
                acc = low[i, j] * t[j, j]
                for m in range(j + 1, i):
                    acc = acc + low[i, m] * t[m, j]
                t[i, j] = -(inv[i] * acc)
        rows = [jnp.broadcast_to(r[j : j + 1], (8, 128)) for j in range(8)]
        new = []
        for k in range(8):
            acc = t[k, 0] * rows[0]
            for j in range(1, k + 1):
                acc = acc + t[k, j] * rows[j]
            new.append(acc)
        out = new[0]
        for k in range(1, 8):
            out = jnp.where(sub == k, new[k], out)
        update = None
        for j in range(8):
            z = t[7, j] * new[7]
            for k in range(j, 7):
                z = z + t[k, j] * new[k]
            c = jnp.stack([lane_pick(v_ref[g], base + j) for g in range(8)])
            term = c * z[None]
            update = term if update is None else update + term
        v = v_ref[...]
        v_ref[...] = jnp.where(group > p, v - update, jnp.where(group == p, out[None], v))
        return 0

    lax.fori_loop(0, 8, panel, 0)


def factor(g_ref, v_ref, ready, after):
    lane = lax.broadcasted_iota(jnp.int32, (64, 128), 1)
    row = lax.broadcasted_iota(jnp.int32, (64, 128), 0)
    lanes = lax.broadcasted_iota(jnp.int32, (64, NB), 1)

    def block(q, _):
        half = lax.rem(q, 2) * 64
        rows = pl.ds(pl.multiple_of(64 * q, 64), 64)
        tile = pl.ds(pl.multiple_of((q // 2) * 128, 128), 128)
        mine = (lane >= half) & (lane < half + 64)
        eye = ((lane - (64 - half)) == row).astype(F32)
        v_ref[...] = jnp.where(mine, g_ref[rows, tile], eye).reshape(8, 8, 128)
        small_inverse(v_ref, half)
        ready(q)
        t = jnp.where(mine, 0.0, v_ref[...].reshape(64, 128))
        gq = g_ref[rows, :]
        u = jnp.dot(t, jnp.concatenate([gq, gq], axis=0), precision=HI, preferred_element_type=F32)
        g_ref[rows, :] = u
        after(q, rows, u)
        left = jnp.where(lanes >= 64 * (q + 1), u[:, :NB], 0.0)
        g_ref[...] -= lax.dot_general(
            left, u, (((0,), (0,)), ((), ())), precision=HI, preferred_element_type=F32
        )
        return 0

    lax.fori_loop(0, 4, block, 0)


def every(*conditions):
    result = conditions[0]
    for condition in conditions[1:]:
        result = result & condition
    return result


def gather_kernel(
    a_ref, w0row, w1row, w0col, w1col, newcol,
    hand_r, hand_c, rraw, craw, linv, w10, low1, a01, a11, g0, g1, v_ref, r1, c1,
    load_sem, h_sem, t_send, t_recv, s_send, s_recv, l_send, l_recv, x_send, x_recv,
):
    row, col = lax.axis_index("row"), lax.axis_index("col")
    x, y, z, k = row // 4, row % 4, col // 2, col % 2

    def device(x, y, z, k):
        return ((x + 4) % 4 * 4 + (y + 4) % 4, (z + 8) % 8 * 2 + (k + 2) % 2)

    def shifted(offset, sign=1):
        dx, dy, dz, dk = offset
        return (
            (x + sign * dx + 4) % 4, (y + sign * dy + 4) % 4,
            (z + sign * dz + 8) % 8, (k + sign * dk + 2) % 2,
        )

    from0 = jnp.where(y == 2, 2, jnp.where(y == 0, 0, 1))
    from1 = jnp.where(y == 3, 2, jnp.where(y == 1, 0, 1))
    back = (4 - x) % 4
    trees = [
        ([((0, 0, 1, 0), lambda x, y, z, k: (k == 1) & (z != 7))], z),
        ([((0, 0, -1, 0), lambda x, y, z, k: (k == 1) & (z != 1))], (8 - z) % 8),
        (
            [
                ((0, 0, 1, 0), lambda x, y, z, k: (k == 1) & (z <= 3)),
                ((0, 0, -1, 0), lambda x, y, z, k: (k == 1) & ((z == 0) | (z >= 6))),
            ],
            jnp.where(z > 4, 8 - z, z),
        ),
        (
            [
                ((-1, 0, 0, 0), lambda x, y, z, k: (k == 1) & (y == 0) & (x != 1)),
                ((0, 1, 0, 0), lambda x, y, z, k: (k == 1) & (y == 0) & (x != 0)),
                ((0, -1, 0, 0), lambda x, y, z, k: (k == 1) & ((y == 0) | (y == 3)) & (x != 0)),
                ((1, 0, 0, 0), lambda x, y, z, k: (k == 1) & (x == 3) & (y != 0)),
            ],
            jnp.where((x == 0) & (y != 0), 2 + from0, back + from0),
        ),
        (
            [
                ((-1, 0, 0, 0), lambda x, y, z, k: (k == 1) & (y != 0) & (x != 1)),
                ((0, 1, 0, 0), lambda x, y, z, k: (k == 1) & jnp.where(x == 0, y == 0, y == 3)),
                ((0, -1, 0, 0), lambda x, y, z, k: (k == 1) & ((y == 0) | (y == 3)) & (x == 0)),
            ],
            jnp.where((x != 0) & (y == 0), 2 + back, back + from0),
        ),
        (
            [
                ((1, 0, 0, 0), lambda x, y, z, k: (k == 1) & (y == 1) & (x != 3)),
                ((0, -1, 0, 0), lambda x, y, z, k: (k == 1) & (y == 1) & (x != 0)),
                ((0, 1, 0, 0), lambda x, y, z, k: (k == 1) & ((y == 1) | (y == 2)) & (x != 0)),
                ((-1, 0, 0, 0), lambda x, y, z, k: (k == 1) & (x == 1) & (y != 1)),
            ],
            jnp.where((x == 0) & (y != 1), 2 + from1, x + from1),
        ),
        (
            [
                ((1, 0, 0, 0), lambda x, y, z, k: (k == 1) & (y != 1) & (x != 3)),
                ((0, -1, 0, 0), lambda x, y, z, k: (k == 1) & jnp.where(x == 0, y == 1, y == 2)),
                ((0, 1, 0, 0), lambda x, y, z, k: (k == 1) & ((y == 1) | (y == 2)) & (x == 0)),
            ],
            jnp.where((x != 0) & (y == 1), 2 + x, x + from1),
        ),
    ]

    def trunk(x, y, k):
        return every(x == 0, y == 0, k == 0)

    def branch(y, k):
        return (y == 0) & (k == 0)

    l_edges = [
        ((0, 0, 2, 0), lambda x, y, z, k: trunk(x, y, k) & ((z == 0) | (z == 2))),
        ((0, 0, 1, 0), lambda x, y, z, k: trunk(x, y, k) & ((z == 0) | (z == 2))),
        ((0, 0, -2, 0), lambda x, y, z, k: trunk(x, y, k) & (z == 0)),
        ((0, 0, -1, 0), lambda x, y, z, k: trunk(x, y, k) & ((z == 0) | (z == 6))),
        ((2, 0, 0, 0), lambda x, y, z, k: trunk(x, y, k)),
        ((1, 0, 0, 0), lambda x, y, z, k: trunk(x, y, k)),
        ((-1, 0, 0, 0), lambda x, y, z, k: trunk(x, y, k)),
        ((0, 2, 0, 0), lambda x, y, z, k: branch(y, k)),
        ((0, 1, 0, 0), lambda x, y, z, k: branch(y, k)),
        ((0, -1, 0, 0), lambda x, y, z, k: branch(y, k)),
        ((0, 0, 0, 1), lambda x, y, z, k: k == 0),
    ]
    corner = every(row == 0, col == 0)
    beside = every(row == 0, col == 1)
    below = every(row == 1, col == 1)
    first, second = k == 0, k == 1
    r_source = z == 0
    c_source = [every(x == 0, y == 0), every(x == 0, y == 1)]
    root = [r_source, r_source, r_source, c_source[0], c_source[0], c_source[1], c_source[1]]

    def r_load(t, dst, lane):
        return pltpu.make_async_copy(
            a_ref.at[:, t, :], dst.at[:, pl.ds(lane + 128 * t, 128)], load_sem.at[t]
        )

    def c_load(t, dst):
        return pltpu.make_async_copy(
            a_ref.at[pl.ds(0, NB), t, :], dst.at[:, pl.ds(128 * t, 128)], load_sem.at[2 + t]
        )

    own = pl.ds(pl.multiple_of(NB * k, NB), NB)

    def loads(act):
        for s in range(2):
            @pl.when(c_source[s] & first)
            def _():
                for t in range(8):
                    act(c_load(t, hand_c))

            @pl.when(c_source[s] & second)
            def _():
                for t in range(8):
                    act(c_load(t, craw.at[s, pl.ds(NB, NB)]))

        @pl.when(r_source & first)
        def _():
            for t in range(2):
                act(r_load(t, hand_r, 0))

        @pl.when(r_source & second)
        def _():
            for t in range(2):
                act(r_load(t, rraw, NB))

    loads(lambda copy: copy.start())

    barrier = pltpu.get_barrier_semaphore()

    def greet(target):
        pl.semaphore_signal(barrier, inc=1, device_id=device(*target), device_id_type=MESH)

    awaited = jnp.where(beside, 2, 1) + jnp.where(below, 1, 0) + jnp.where(corner, 1, 0)
    greet((x, y, z, 1 - k))
    for offset, sends in [edge for edges, _ in trees for edge in edges] + l_edges[:-1]:
        awaited = awaited + sends(x, y, z, k).astype(jnp.int32)
        parent = shifted(offset, -1)

        @pl.when(sends(*parent))
        def _():
            greet(parent)

    @pl.when(corner)
    def _():
        greet((0, 0, 0, 1))
        greet((0, 1, 0, 1))

    @pl.when(below)
    def _():
        greet((0, 0, 0, 0))

    linv[0, pl.ds(0, 128), pl.ds(128, 128)] = jnp.zeros((128, 128), F32)
    linv[1, pl.ds(0, 128), pl.ds(128, 128)] = jnp.zeros((128, 128), F32)
    pl.semaphore_wait(barrier, awaited)

    def remote(src, dst, send, recv, target):
        return pltpu.make_async_remote_copy(
            src_ref=src, dst_ref=dst, send_sem=send, recv_sem=recv,
            device_id=target, device_id_type=MESH,
        )

    t_on = [[sends(x, y, z, k) for _, sends in edges] for edges, _ in trees]
    t_to = [[device(*shifted(offset)) for offset, _ in edges] for edges, _ in trees]
    l_on = [sends(x, y, z, k) for _, sends in l_edges]
    l_to = [device(*shifted(offset)) for offset, _ in l_edges]
    sibling = device(x, y, z, 1 - k)
    first_step = [PARTS[u][3] + HOP * depth for u, (_, depth) in enumerate(trees)]

    def t_ref(u, start, count):
        rows, top, _, _ = PARTS[u]
        span = pl.ds(pl.multiple_of(top + rows * start, rows), rows * count)
        return rraw.at[span, :] if u < 3 else craw.at[(u - 3) // 2, span, :]

    def t_copy(u, n, e=0):
        part = t_ref(u, 0, PARTS[u][2]) if n is None else t_ref(u, n, 1)
        return remote(part, part, t_send.at[u, e], t_recv.at[u, 0 if n is None else n], t_to[u][e])

    def s_copy(u, i):
        part = t_ref(u, 4 * i, 4)
        return remote(part, part, s_send.at[u, i], s_recv.at[u, i], sibling)

    for_first = (0, 1, 2, 3, 5)

    def h_copy(i):
        if i < 2:
            src, dst = hand_r.at[pl.ds(512 * i, 512), :], rraw.at[pl.ds(512 * i, 512), pl.ds(0, NB)]
        else:
            half = pl.ds(128 * (i - 2), 128)
            src, dst = hand_c.at[half, :], craw.at[row % 2, half, :]
        return remote(src, dst, h_sem.at[0, i], h_sem.at[1, i], sibling)

    pieces = [
        linv.at[0, pl.ds(0, 128), pl.ds(0, 128)],
        linv.at[0, pl.ds(128, 128), :],
        w10,
        linv.at[1, pl.ds(0, 128), pl.ds(0, 128)],
        linv.at[1, pl.ds(128, 64), :],
        linv.at[1, pl.ds(192, 64), :],
    ]

    def l_copy(p, e):
        return remote(pieces[p], pieces[p], l_send.at[p, e], l_recv.at[p], l_to[e])

    def send_piece(p):
        for e, on in enumerate(l_on):
            @pl.when(on)
            def _():
                l_copy(p, e).start()

    def wait_pieces(some):
        for p in some:
            l_copy(p, 0).wait_recv()

    def pass_pieces(some):
        for p in some:
            l_copy(p, 0).wait_recv()
            send_piece(p)

    def a01_copy():
        return remote(craw.at[0, pl.ds(NB, NB), pl.ds(0, NB)], a01, x_send.at[0], x_recv.at[0], (0, 0))

    def a11_copy():
        return remote(craw.at[1, pl.ds(NB, NB), pl.ds(0, NB)], a11, x_send.at[1], x_recv.at[1], (0, 0))

    def low1_copy():
        return remote(low1, low1, x_send.at[2], x_recv.at[2], (1, 1))

    loads(lambda copy: copy.wait())

    @pl.when(beside)
    def _():
        a01_copy().start()

    @pl.when(below)
    def _():
        a11_copy().start()

    c_root = c_source[0] | c_source[1]
    halves = [r_source, r_source, c_root, c_root]
    for i in (0, 2, 1, 3):
        @pl.when(halves[i] & first)
        def _():
            h_copy(i).start()

    @pl.when(corner)
    def _():
        eye = (
            lax.broadcasted_iota(jnp.int32, (NB, NB), 0) == lax.broadcasted_iota(jnp.int32, (NB, NB), 1)
        ).astype(F32)
        g0[:, :NB] = hand_c[:, :NB]
        g0[:, 2 * NB :] = eye
        g1[:, NB:] = eye

        def ready0(q):
            @pl.when(q == 0)
            def _():
                a01_copy().wait_recv()
                g0[:, NB : 2 * NB] = a01[...]
                a11_copy().wait_recv()
                g1[:, :NB] = a11[...]

        def after0(q, rows, u):
            linv[0, rows, :] = u[:, 2 * NB :]
            w = u[:, NB : 2 * NB].astype(BF16)
            w10[rows, :] = w
            g1[:, :NB] -= lax.dot_general(w, w, (((0,), (0,)), ((), ())), preferred_element_type=F32)

            @pl.when(q == 1)
            def _():
                send_piece(0)

            @pl.when(q == 3)
            def _():
                send_piece(1)
                send_piece(2)

        factor(g0, v_ref, ready0, after0)

        def after1(q, rows, u):
            linv[1, rows, :] = u[:, NB:]
            low1[rows, :] = u[:, :NB]
            for i in range(3):
                @pl.when(q == i + 1)
                def _():
                    send_piece(3 + i)

        factor(g1, v_ref, lambda q: None, after1)
        low1_copy().start()

    @pl.when(first & jnp.logical_not(corner))
    def _():
        pass_pieces((0, 1, 2))

    @pl.when(branch(y, k) & jnp.logical_not(corner))
    def _():
        pass_pieces((3, 4, 5))

    @pl.when(second)
    def _():
        def step(m, _):
            for i in range(4):
                @pl.when(halves[i] & (m == 8 * (i % 2)))
                def _():
                    h_copy(i).wait_recv()

            for u in range(7):
                n = m - first_step[u]

                @pl.when((n >= 0) & (n < PARTS[u][2]))
                def _():
                    @pl.when(jnp.logical_not(root[u]))
                    def _():
                        t_copy(u, n).wait_recv()

                    for e, on in enumerate(t_on[u]):
                        @pl.when(on)
                        def _():
                            t_copy(u, n, e).start()

                    if u in for_first:
                        @pl.when(n % 4 == 3)
                        def _():
                            s_copy(u, n // 4).start()

            return 0

        lax.fori_loop(0, 40, step, 0)
        wait_pieces((0, 1, 2))

    @pl.when(first)
    def _():
        for u in for_first:
            for i in range(PARTS[u][2] // 4):
                s_copy(u, i).wait_recv()

    upper = lax.broadcasted_iota(jnp.int32, (NB, NB), 1) > lax.broadcasted_iota(jnp.int32, (NB, NB), 0)
    nt = (((1,), (1,)), ((), ()))
    tn = (((0,), (0,)), ((), ()))
    for b in range(4):
        rows = pl.ds(NB * b, NB)
        solved = lax.dot_general(
            rraw[rows, pl.ds(0, NB)], linv[0], nt, precision=HI, preferred_element_type=F32
        )
        newcol[rows, :] = solved
        rounded = solved.astype(BF16)
        if b == 0:
            rounded = jnp.where(row == 0, jnp.zeros_like(rounded), rounded)
        w0row[rows, :] = rounded
        r1[rows, :] = rraw[rows, pl.ds(NB, NB)] - jnp.dot(rounded, w10[...], preferred_element_type=F32)
        solved = jnp.dot(linv[0], craw[0, own, rows], precision=HI, preferred_element_type=F32)
        rounded = solved.astype(BF16)
        if b == 0:
            rounded = jnp.where(col == 0, jnp.zeros_like(rounded), rounded)
        w0col[:, rows] = rounded
        c1[:, rows] = craw[1, own, rows] - lax.dot_general(
            w10[...], rounded, tn, preferred_element_type=F32
        )

    @pl.when(first & (y != 0))
    def _():
        pass_pieces((3, 4, 5))

    @pl.when(second)
    def _():
        wait_pieces((3, 4, 5))

    for b in range(4):
        rows = pl.ds(NB * b, NB)
        solved = lax.dot_general(r1[rows, :], linv[1], nt, precision=HI, preferred_element_type=F32)
        rounded = solved.astype(BF16)
        if b == 0:
            rounded = jnp.where(row <= 1, jnp.zeros_like(rounded), rounded)
            solved = jnp.where(row == 0, r1[rows, :], solved)
        w1row[rows, :] = rounded

        @pl.when(col == 1)
        def _():
            newcol[rows, :] = solved

        solved = jnp.dot(linv[1], c1[:, rows], precision=HI, preferred_element_type=F32)
        rounded = solved.astype(BF16)
        if b == 0:
            rounded = jnp.where(col <= 1, jnp.zeros_like(rounded), rounded)
        w1col[:, rows] = rounded

    @pl.when(corner)
    def _():
        newcol[pl.ds(0, NB), :] = jnp.where(upper, 0.0, g0[:, :NB].T)

    @pl.when(below)
    def _():
        low1_copy().wait_recv()
        newcol[pl.ds(0, NB), :] = jnp.where(upper, 0.0, low1[...].T)

    for u in range(7):
        for e, on in enumerate(t_on[u]):
            @pl.when(on)
            def _():
                t_copy(u, None, e).wait_send()

    @pl.when(second)
    def _():
        for u in for_first:
            for i in range(PARTS[u][2] // 4):
                s_copy(u, i).wait_send()

    for i in range(4):
        @pl.when(halves[i] & first)
        def _():
            h_copy(i).wait_send()

    for e, on in enumerate(l_on):
        @pl.when(on)
        def _():
            for p in range(6):
                l_copy(p, e).wait_send()

    @pl.when(beside)
    def _():
        a01_copy().wait_send()

    @pl.when(below)
    def _():
        a11_copy().wait_send()

    @pl.when(corner)
    def _():
        low1_copy().wait_send()


def trailing_kernel(a_ref, w0row, w1row, w0col, w1col, newcol, o_ref):
    col = lax.axis_index("col")
    update = jnp.dot(w0row[...], w0col[...], preferred_element_type=F32)
    update += jnp.dot(w1row[...], w1col[...], preferred_element_type=F32)
    for t in range(8):
        part = a_ref[:, t, :] - update[:, 128 * t : 128 * (t + 1)]
        if t < 2:
            part = jnp.where(col <= 1, newcol[:, 128 * t : 128 * (t + 1)], part)
        o_ref[:, t, :] = part


def on_device(covariance):
    shape = covariance.shape
    a = covariance.reshape(1024, 8, 128)
    vmem = pl.BlockSpec(memory_space=pltpu.VMEM)
    dma = pltpu.SemaphoreType.DMA
    panels = pl.pallas_call(
        gather_kernel,
        out_shape=(
            jax.ShapeDtypeStruct((1024, NB), BF16),
            jax.ShapeDtypeStruct((1024, NB), BF16),
            jax.ShapeDtypeStruct((NB, 1024), BF16),
            jax.ShapeDtypeStruct((NB, 1024), BF16),
            jax.ShapeDtypeStruct((1024, NB), F32),
        ),
        in_specs=[pl.BlockSpec(memory_space=pl.ANY)],
        out_specs=(vmem,) * 5,
        scratch_shapes=[
            pltpu.VMEM((1024, NB), F32),
            pltpu.VMEM((NB, 1024), F32),
            pltpu.VMEM((1024, 2 * NB), F32),
            pltpu.VMEM((2, 2 * NB, 1024), F32),
            pltpu.VMEM((2, NB, NB), F32),
            pltpu.VMEM((NB, NB), BF16),
            pltpu.VMEM((NB, NB), F32),
            pltpu.VMEM((NB, NB), F32),
            pltpu.VMEM((NB, NB), F32),
            pltpu.VMEM((NB, 3 * NB), F32),
            pltpu.VMEM((NB, 2 * NB), F32),
            pltpu.VMEM((8, 8, 128), F32),
            pltpu.VMEM((1024, NB), F32),
            pltpu.VMEM((NB, 1024), F32),
            dma((10,)),
            dma((2, 4)),
            dma((7, 4)),
            dma((7, 16)),
            dma((7, 4)),
            dma((7, 4)),
            dma((6, 11)),
            dma((6,)),
            dma((3,)),
            dma((3,)),
        ],
        compiler_params=pltpu.CompilerParams(
            collective_id=0, has_side_effects=True, vmem_limit_bytes=48 << 20
        ),
        name="panels",
    )(a)
    steps = 8
    rows = 1024 // steps
    out = pl.pallas_call(
        trailing_kernel,
        grid=(steps,),
        out_shape=jax.ShapeDtypeStruct((1024, 8, 128), F32),
        in_specs=[
            pl.BlockSpec((rows, 8, 128), lambda i: (i, 0, 0)),
            pl.BlockSpec((rows, NB), lambda i: (i, 0)),
            pl.BlockSpec((rows, NB), lambda i: (i, 0)),
            pl.BlockSpec((NB, 1024), lambda i: (0, 0)),
            pl.BlockSpec((NB, 1024), lambda i: (0, 0)),
            pl.BlockSpec((rows, NB), lambda i: (i, 0)),
        ],
        out_specs=pl.BlockSpec((rows, 8, 128), lambda i: (i, 0, 0)),
        compiler_params=pltpu.CompilerParams(vmem_limit_bytes=32 << 20),
        name="trailing",
    )(a, *panels)
    return out.reshape(shape)


def solution(mesh):
    spec = P(None, "row", None, None, "col", None)
    return jax.shard_map(
        on_device, mesh=mesh, in_specs=(spec,), out_specs=spec, check_vma=False
    )
```

```python
import jax
import jax.numpy as jnp
from jax import lax
from jax.experimental import pallas as pl
from jax.experimental.pallas import tpu as pltpu
from jax.sharding import PartitionSpec as P

MESH = pl.DeviceIdType.MESH
HI = lax.Precision.HIGHEST
F32 = jnp.float32
BF16 = jnp.bfloat16
NB = 256
R_PARTS = [(32, 0, 8, 0), (32, 256, 8, 0), (32, 512, 16, 8)]
C_PARTS = [(16, 0, 16, 0), (16, 256, 16, 0)]
PARTS = R_PARTS + C_PARTS + C_PARTS
HOP = 4
EARLY = 5
PIECES = 8


def product(a, b, dims):
    high_a, high_b = a.astype(BF16), b.astype(BF16)
    low_a, low_b = (a - high_a.astype(F32)).astype(BF16), (b - high_b.astype(F32)).astype(BF16)

    def dot(p, q):
        return lax.dot_general(p, q, dims, preferred_element_type=F32)

    return dot(high_a, high_b) + (dot(high_a, low_b) + dot(low_a, high_b))


def lane_pick(value, lane):
    return jnp.take_along_axis(value, jnp.full(value.shape, lane, jnp.int32), axis=1)


def small_inverse(v_ref, half):
    group = lax.broadcasted_iota(jnp.int32, (8, 8, 128), 0)
    sub = lax.broadcasted_iota(jnp.int32, (8, 128), 0)

    def panel(p, _):
        r = v_ref[p]
        base = 8 * p + half
        s, low, t, inv = {}, {}, {}, []
        for k in range(8):
            c = lane_pick(r, base + k)
            for i in range(k, 8):
                s[i, k] = jnp.broadcast_to(c[i : i + 1], (8, 128))
        for k in range(8):
            rk = lax.rsqrt(s[k, k])
            inv.append(rk)
            for i in range(k + 1, 8):
                low[i, k] = s[i, k] * rk
            for j in range(k + 1, 8):
                for i in range(j, 8):
                    s[i, j] = s[i, j] - low[i, k] * low[j, k]
        for i in range(8):
            t[i, i] = inv[i]
            for j in range(i):
                acc = low[i, j] * t[j, j]
                for m in range(j + 1, i):
                    acc = acc + low[i, m] * t[m, j]
                t[i, j] = -(inv[i] * acc)
        rows = [jnp.broadcast_to(r[j : j + 1], (8, 128)) for j in range(8)]
        new = []
        for k in range(8):
            acc = t[k, 0] * rows[0]
            for j in range(1, k + 1):
                acc = acc + t[k, j] * rows[j]
            new.append(acc)
        out = new[0]
        for k in range(1, 8):
            out = jnp.where(sub == k, new[k], out)
        update = None
        for j in range(8):
            z = t[7, j] * new[7]
            for k in range(j, 7):
                z = z + t[k, j] * new[k]
            c = jnp.stack([lane_pick(v_ref[g], base + j) for g in range(8)])
            term = c * z[None]
            update = term if update is None else update + term
        v = v_ref[...]
        v_ref[...] = jnp.where(group > p, v - update, jnp.where(group == p, out[None], v))
        return 0

    lax.fori_loop(0, 8, panel, 0)


def invert_block(g_ref, v_ref, q):
    lane = lax.broadcasted_iota(jnp.int32, (64, 128), 1)
    row = lax.broadcasted_iota(jnp.int32, (64, 128), 0)
    half = (q % 2) * 64
    rows = pl.ds(pl.multiple_of(64 * q, 64), 64)
    tile = pl.ds(pl.multiple_of((q // 2) * 128, 128), 128)
    mine = (lane >= half) & (lane < half + 64)
    eye = ((lane - (64 - half)) == row).astype(F32)
    v_ref[...] = jnp.where(mine, g_ref[rows, tile], eye).reshape(8, 8, 128)
    small_inverse(v_ref, half)


def factor(g_ref, v_ref, ready, after):
    lane = lax.broadcasted_iota(jnp.int32, (64, 128), 1)
    lanes = lax.broadcasted_iota(jnp.int32, (64, NB), 1)

    def block(q, _):
        half = lax.rem(q, 2) * 64
        rows = pl.ds(pl.multiple_of(64 * q, 64), 64)
        mine = (lane >= half) & (lane < half + 64)

        @pl.when(q > 0)
        def _():
            invert_block(g_ref, v_ref, q)

        ready(q)
        t = jnp.where(mine, 0.0, v_ref[...].reshape(64, 128))
        gq = g_ref[rows, :]
        u = jnp.dot(t, jnp.concatenate([gq, gq], axis=0), precision=HI, preferred_element_type=F32)
        g_ref[rows, :] = u
        after(q, rows, u)
        left = jnp.where(lanes >= 64 * (q + 1), u[:, :NB], 0.0)

        @pl.when(q < 3)
        def _():
            g_ref[...] -= lax.dot_general(
                left, u, (((0,), (0,)), ((), ())), precision=HI, preferred_element_type=F32
            )

        return 0

    lax.fori_loop(0, 4, block, 0)


def every(*conditions):
    result = conditions[0]
    for condition in conditions[1:]:
        result = result & condition
    return result


def gather_kernel(
    a_ref, w0row, w1row, w0col, w1col, newcol,
    hand_r, hand_c, rraw, craw, linv, w10, low1, a01, a11, g0, g1, v_ref, r1, c1,
    load_sem, h_sem, t_send, t_recv, s_send, s_recv, l_send, l_recv, x_send, x_recv,
):
    row, col = lax.axis_index("row"), lax.axis_index("col")
    x, y, z, k = row // 4, row % 4, col // 2, col % 2

    def device(x, y, z, k):
        return ((x + 4) % 4 * 4 + (y + 4) % 4, (z + 8) % 8 * 2 + (k + 2) % 2)

    def shifted(offset, sign=1):
        dx, dy, dz, dk = offset
        return (
            (x + sign * dx + 4) % 4, (y + sign * dy + 4) % 4,
            (z + sign * dz + 8) % 8, (k + sign * dk + 2) % 2,
        )

    from0 = jnp.where(y == 2, 2, jnp.where(y == 0, 0, 1))
    from1 = jnp.where(y == 3, 2, jnp.where(y == 1, 0, 1))
    back = (4 - x) % 4
    trees = [
        ([((0, 0, 1, 0), lambda x, y, z, k: (k == 1) & (z != 7))], z),
        ([((0, 0, -1, 0), lambda x, y, z, k: (k == 1) & (z != 1))], (8 - z) % 8),
        (
            [
                ((0, 0, 1, 0), lambda x, y, z, k: (k == 1) & (z <= 3)),
                ((0, 0, -1, 0), lambda x, y, z, k: (k == 1) & ((z == 0) | (z >= 6))),
            ],
            jnp.where(z > 4, 8 - z, z),
        ),
        (
            [
                ((-1, 0, 0, 0), lambda x, y, z, k: (k == 1) & (y == 0) & (x != 1)),
                ((0, 1, 0, 0), lambda x, y, z, k: (k == 1) & (y == 0) & (x != 0)),
                ((0, -1, 0, 0), lambda x, y, z, k: (k == 1) & ((y == 0) | (y == 3)) & (x != 0)),
                ((1, 0, 0, 0), lambda x, y, z, k: (k == 1) & (x == 3) & (y != 0)),
            ],
            jnp.where((x == 0) & (y != 0), 2 + from0, back + from0),
        ),
        (
            [
                ((-1, 0, 0, 0), lambda x, y, z, k: (k == 1) & (y != 0) & (x != 1)),
                ((0, 1, 0, 0), lambda x, y, z, k: (k == 1) & jnp.where(x == 0, y == 0, y == 3)),
                ((0, -1, 0, 0), lambda x, y, z, k: (k == 1) & ((y == 0) | (y == 3)) & (x == 0)),
            ],
            jnp.where((x != 0) & (y == 0), 2 + back, back + from0),
        ),
        (
            [
                ((1, 0, 0, 0), lambda x, y, z, k: (k == 1) & (y == 1) & (x != 3)),
                ((0, -1, 0, 0), lambda x, y, z, k: (k == 1) & (y == 1) & (x != 0)),
                ((0, 1, 0, 0), lambda x, y, z, k: (k == 1) & ((y == 1) | (y == 2)) & (x != 0)),
                ((-1, 0, 0, 0), lambda x, y, z, k: (k == 1) & (x == 1) & (y != 1)),
            ],
            jnp.where((x == 0) & (y != 1), 2 + from1, x + from1),
        ),
        (
            [
                ((1, 0, 0, 0), lambda x, y, z, k: (k == 1) & (y != 1) & (x != 3)),
                ((0, -1, 0, 0), lambda x, y, z, k: (k == 1) & jnp.where(x == 0, y == 1, y == 2)),
                ((0, 1, 0, 0), lambda x, y, z, k: (k == 1) & ((y == 1) | (y == 2)) & (x == 0)),
            ],
            jnp.where((x != 0) & (y == 1), 2 + x, x + from1),
        ),
    ]

    def branch(y, k):
        return (y == 0) & (k == 0)

    def entry(z):
        return jnp.where(z == 4, 2, jnp.where((z == 2) | (z == 6), 1, jnp.where((z == 3) | (z == 5), 3, 0)))

    def along_z(at):
        return lambda x, y, z, k: branch(y, k) & (z == 0) & (x == at)

    def along_x(x, y, z, k):
        return branch(y, k) & (x == entry(z))

    def along_y(x, y, z, k):
        return branch(y, k)

    l_edges = [
        ((2, 0, 0, 0), along_x),
        ((1, 0, 0, 0), along_x),
        ((-1, 0, 0, 0), along_x),
        ((0, 0, 1, 0), along_z(0)),
        ((0, 0, -1, 0), along_z(0)),
        ((0, 0, 2, 0), along_z(1)),
        ((0, 0, -2, 0), along_z(1)),
        ((0, 0, 4, 0), along_z(2)),
        ((0, 0, 3, 0), along_z(3)),
        ((0, 0, -3, 0), along_z(3)),
        ((0, 2, 0, 0), along_y),
        ((0, 1, 0, 0), along_y),
        ((0, -1, 0, 0), along_y),
        ((0, 0, 0, 1), lambda x, y, z, k: k == 0),
    ]
    corner = every(row == 0, col == 0)
    beside = every(row == 0, col == 1)
    below = every(row == 1, col == 1)
    first, second = k == 0, k == 1
    r_source = z == 0
    c_source = [every(x == 0, y == 0), every(x == 0, y == 1)]
    root = [r_source, r_source, r_source, c_source[0], c_source[0], c_source[1], c_source[1]]

    def r_load(t, dst, lane):
        return pltpu.make_async_copy(
            a_ref.at[:, t, :], dst.at[:, pl.ds(lane + 128 * t, 128)], load_sem.at[t]
        )

    def c_load(t, dst):
        return pltpu.make_async_copy(
            a_ref.at[pl.ds(0, NB), t, :], dst.at[:, pl.ds(128 * t, 128)], load_sem.at[2 + t]
        )

    own = pl.ds(pl.multiple_of(NB * k, NB), NB)

    def c_loads(act, some):
        for s in range(2):
            @pl.when(c_source[s] & first)
            def _():
                for t in some:
                    act(c_load(t, hand_c))

            @pl.when(c_source[s] & second)
            def _():
                for t in some:
                    act(c_load(t, craw.at[s, pl.ds(NB, NB)]))

    def r_loads(act):
        @pl.when(r_source)
        def _():
            for t in range(2):
                act(r_load(t, hand_r, 0))

    c_loads(lambda copy: copy.start(), range(8))
    r_loads(lambda copy: copy.start())

    barrier = pltpu.get_barrier_semaphore()

    def greet(target):
        pl.semaphore_signal(barrier, inc=1, device_id=device(*target), device_id_type=MESH)

    awaited = jnp.where(beside, 2, 1) + jnp.where(below, 1, 0) + jnp.where(corner, 1, 0)
    greet((x, y, z, 1 - k))
    for offset, sends in [edge for edges, _ in trees for edge in edges] + l_edges[:-1]:
        awaited = awaited + sends(x, y, z, k).astype(jnp.int32)
        parent = shifted(offset, -1)

        @pl.when(sends(*parent))
        def _():
            greet(parent)

    @pl.when(corner)
    def _():
        greet((0, 0, 0, 1))
        greet((0, 1, 0, 1))

    @pl.when(below)
    def _():
        greet((0, 0, 0, 0))

    linv[0, pl.ds(0, 128), pl.ds(128, 128)] = jnp.zeros((128, 128), F32)
    linv[1, pl.ds(0, 128), pl.ds(128, 128)] = jnp.zeros((128, 128), F32)
    c_loads(lambda copy: copy.wait(), range(2))

    @pl.when(corner)
    def _():
        eye = (
            lax.broadcasted_iota(jnp.int32, (NB, NB), 0) == lax.broadcasted_iota(jnp.int32, (NB, NB), 1)
        ).astype(F32)
        g0[:, :NB] = hand_c[:, :NB]
        g0[:, 2 * NB :] = eye
        g1[:, :NB] = jnp.zeros((NB, NB), F32)
        g1[:, NB:] = eye
        invert_block(g0, v_ref, 0)

    pl.semaphore_wait(barrier, awaited)

    def remote(src, dst, send, recv, target):
        return pltpu.make_async_remote_copy(
            src_ref=src, dst_ref=dst, send_sem=send, recv_sem=recv,
            device_id=target, device_id_type=MESH,
        )

    t_on = [[sends(x, y, z, k) for _, sends in edges] for edges, _ in trees]
    t_to = [[device(*shifted(offset)) for offset, _ in edges] for edges, _ in trees]
    l_on = [sends(x, y, z, k) for _, sends in l_edges]
    l_to = [device(*shifted(offset)) for offset, _ in l_edges]
    sibling = device(x, y, z, 1 - k)
    first_step = [PARTS[u][3] + HOP * depth for u, (_, depth) in enumerate(trees)]

    def t_ref(u, start, count):
        rows, top, _, _ = PARTS[u]
        span = pl.ds(pl.multiple_of(top + rows * start, rows), rows * count)
        return rraw.at[span, :] if u < 3 else craw.at[(u - 3) // 2, span, :]

    def t_copy(u, n, e=0):
        part = t_ref(u, 0, PARTS[u][2]) if n is None else t_ref(u, n, 1)
        return remote(part, part, t_send.at[u, e], t_recv.at[u, 0 if n is None else n], t_to[u][e])

    def s_copy(u, i):
        part = t_ref(u, 4 * i, 4)
        return remote(part, part, s_send.at[u, i], s_recv.at[u, i], sibling)

    for_first = (0, 1, 2, 3, 5)

    def h_copy(i):
        if i < 2:
            src, dst = hand_r.at[pl.ds(512 * i, 512), :], rraw.at[pl.ds(512 * i, 512), pl.ds(0, NB)]
        else:
            half = pl.ds(128 * (i - 2), 128)
            src, dst = hand_c.at[half, :], craw.at[row % 2, half, :]
        return remote(src, dst, h_sem.at[0, i], h_sem.at[1, i], sibling)

    pieces = [
        linv.at[0, pl.ds(0, 128), pl.ds(0, 128)],
        w10.at[pl.ds(0, 128), :],
        linv.at[0, pl.ds(128, 64), :],
        linv.at[0, pl.ds(192, 64), :],
        w10.at[pl.ds(128, 128), :],
        linv.at[1, pl.ds(0, 128), pl.ds(0, 128)],
        linv.at[1, pl.ds(128, 64), :],
        linv.at[1, pl.ds(192, 64), :],
    ]

    def l_copy(p, e):
        return remote(pieces[p], pieces[p], l_send.at[p, e], l_recv.at[p], l_to[e])

    def send_piece(p):
        for e, on in enumerate(l_on):
            @pl.when(on)
            def _():
                l_copy(p, e).start()

    def wait_pieces(some):
        for p in some:
            l_copy(p, 0).wait_recv()

    def pass_pieces(some):
        for p in some:
            l_copy(p, 0).wait_recv()
            send_piece(p)

    def a01_copy():
        return remote(craw.at[0, pl.ds(NB, NB), pl.ds(0, NB)], a01, x_send.at[0], x_recv.at[0], (0, 0))

    def a11_copy():
        return remote(craw.at[1, pl.ds(NB, NB), pl.ds(0, NB)], a11, x_send.at[1], x_recv.at[1], (0, 0))

    def low1_copy():
        return remote(low1, low1, x_send.at[2], x_recv.at[2], (1, 1))

    @pl.when(beside)
    def _():
        a01_copy().start()

    @pl.when(below)
    def _():
        a11_copy().start()

    c_root = c_source[0] | c_source[1]
    halves = [r_source, r_source, c_root, c_root]

    def hand_over():
        c_loads(lambda copy: copy.wait(), range(2, 8))
        r_loads(lambda copy: copy.wait())
        for i in (0, 2, 1, 3):
            @pl.when(halves[i] & first)
            def _():
                h_copy(i).start()

    hand_over()

    @pl.when(r_source & second)
    def _():
        rraw[:, NB:] = hand_r[...]

    @pl.when(corner)
    def _():
        def ready0(q):
            @pl.when(q == 0)
            def _():
                a01_copy().wait_recv()
                g0[:, NB : 2 * NB] = a01[...]

        def after0(q, rows, u):
            linv[0, rows, :] = u[:, 2 * NB :]
            w = u[:, NB : 2 * NB].astype(BF16)
            w10[rows, :] = w
            g1[:, :NB] -= lax.dot_general(w, w, (((0,), (0,)), ((), ())), preferred_element_type=F32)

            @pl.when(q == 1)
            def _():
                send_piece(0)
                send_piece(1)

            @pl.when(q == 2)
            def _():
                send_piece(2)

            @pl.when(q == 3)
            def _():
                send_piece(3)
                send_piece(4)

        factor(g0, v_ref, ready0, after0)
        a11_copy().wait_recv()
        g1[:, :NB] += a11[...]
        invert_block(g1, v_ref, 0)

        def after1(q, rows, u):
            linv[1, rows, :] = u[:, NB:]
            low1[rows, :] = u[:, :NB]
            for i in range(3):
                @pl.when(q == i + 1)
                def _():
                    send_piece(EARLY + i)

        factor(g1, v_ref, lambda q: None, after1)
        low1_copy().start()

    @pl.when(first & jnp.logical_not(corner))
    def _():
        pass_pieces(range(EARLY))

    @pl.when(branch(y, k) & jnp.logical_not(corner))
    def _():
        pass_pieces(range(EARLY, PIECES))

    @pl.when(second)
    def _():
        def step(m, _):
            for i in range(4):
                @pl.when(halves[i] & (m == 8 * (i % 2)))
                def _():
                    h_copy(i).wait_recv()

            for u in range(7):
                n = m - first_step[u]

                @pl.when((n >= 0) & (n < PARTS[u][2]))
                def _():
                    @pl.when(jnp.logical_not(root[u]))
                    def _():
                        t_copy(u, n).wait_recv()

                    for e, on in enumerate(t_on[u]):
                        @pl.when(on)
                        def _():
                            t_copy(u, n, e).start()

                    if u in for_first:
                        @pl.when(n % 4 == 3)
                        def _():
                            s_copy(u, n // 4).start()

            return 0

        lax.fori_loop(0, 40, step, 0)
        wait_pieces(range(EARLY))

    def wait_parts(u, some):
        @pl.when(first)
        def _():
            for i in some:
                s_copy(u, i).wait_recv()

    upper = lax.broadcasted_iota(jnp.int32, (NB, NB), 1) > lax.broadcasted_iota(jnp.int32, (NB, NB), 0)
    nn = (((1,), (0,)), ((), ()))
    nt = (((1,), (1,)), ((), ()))
    tn = (((0,), (0,)), ((), ()))
    for b in range(4):
        rows = pl.ds(NB * b, NB)
        wait_parts(min(b, 2), range(2 * (b // 3), 2 + 2 * (b // 3)))
        solved = product(rraw[rows, pl.ds(0, NB)], linv[0], nt)
        newcol[rows, :] = solved
        rounded = solved.astype(BF16)
        if b == 0:
            rounded = jnp.where(row == 0, jnp.zeros_like(rounded), rounded)
        w0row[rows, :] = rounded
        r1[rows, :] = rraw[rows, pl.ds(NB, NB)] - jnp.dot(rounded, w10[...], preferred_element_type=F32)
    wait_parts(3, range(4))
    wait_parts(5, range(4))
    for b in range(4):
        rows = pl.ds(NB * b, NB)
        solved = product(linv[0], craw[0, own, rows], nn)
        rounded = solved.astype(BF16)
        if b == 0:
            rounded = jnp.where(col == 0, jnp.zeros_like(rounded), rounded)
        w0col[:, rows] = rounded
        c1[:, rows] = craw[1, own, rows] - lax.dot_general(
            w10[...], rounded, tn, preferred_element_type=F32
        )

    @pl.when(first & (y != 0))
    def _():
        pass_pieces(range(EARLY, PIECES))

    @pl.when(second)
    def _():
        wait_pieces(range(EARLY, PIECES))

    for b in range(4):
        rows = pl.ds(NB * b, NB)
        solved = product(r1[rows, :], linv[1], nt)
        rounded = solved.astype(BF16)
        if b == 0:
            rounded = jnp.where(row <= 1, jnp.zeros_like(rounded), rounded)
            solved = jnp.where(row == 0, r1[rows, :], solved)
        w1row[rows, :] = rounded

        @pl.when(col == 1)
        def _():
            newcol[rows, :] = solved

        solved = product(linv[1], c1[:, rows], nn)
        rounded = solved.astype(BF16)
        if b == 0:
            rounded = jnp.where(col <= 1, jnp.zeros_like(rounded), rounded)
        w1col[:, rows] = rounded

    @pl.when(corner)
    def _():
        newcol[pl.ds(0, NB), :] = jnp.where(upper, 0.0, g0[:, :NB].T)

    @pl.when(below)
    def _():
        low1_copy().wait_recv()
        newcol[pl.ds(0, NB), :] = jnp.where(upper, 0.0, low1[...].T)

    for u in range(7):
        for e, on in enumerate(t_on[u]):
            @pl.when(on)
            def _():
                t_copy(u, None, e).wait_send()

    @pl.when(second)
    def _():
        for u in for_first:
            for i in range(PARTS[u][2] // 4):
                s_copy(u, i).wait_send()

    for i in range(4):
        @pl.when(halves[i] & first)
        def _():
            h_copy(i).wait_send()

    for p in range(PIECES):
        for e, on in enumerate(l_on):
            @pl.when(on)
            def _():
                l_copy(p, e).wait_send()

    @pl.when(beside)
    def _():
        a01_copy().wait_send()

    @pl.when(below)
    def _():
        a11_copy().wait_send()

    @pl.when(corner)
    def _():
        low1_copy().wait_send()


def trailing_kernel(a_ref, w0row, w1row, w0col, w1col, newcol, o_ref):
    count = o_ref.shape[0]
    rows = pl.ds(pl.multiple_of(pl.program_id(0) * count, count), count)
    update = jnp.dot(w0row[rows, :], w0col[...], preferred_element_type=F32)
    update += jnp.dot(w1row[rows, :], w1col[...], preferred_element_type=F32)
    o_ref[...] = a_ref[rows] - update.reshape(count, 8, 128)

    @pl.when(lax.axis_index("col") <= 1)
    def _():
        for t in range(2):
            o_ref[:, t, :] = newcol[rows, pl.ds(128 * t, 128)]


def on_device(covariance):
    shape = covariance.shape
    a = covariance.reshape(1024, 8, 128)
    vmem = pl.BlockSpec(memory_space=pltpu.VMEM)
    dma = pltpu.SemaphoreType.DMA
    panels = pl.pallas_call(
        gather_kernel,
        out_shape=(
            jax.ShapeDtypeStruct((1024, NB), BF16),
            jax.ShapeDtypeStruct((1024, NB), BF16),
            jax.ShapeDtypeStruct((NB, 1024), BF16),
            jax.ShapeDtypeStruct((NB, 1024), BF16),
            jax.ShapeDtypeStruct((1024, NB), F32),
        ),
        in_specs=[pl.BlockSpec(memory_space=pl.ANY)],
        out_specs=(vmem,) * 5,
        scratch_shapes=[
            pltpu.VMEM((1024, NB), F32),
            pltpu.VMEM((NB, 1024), F32),
            pltpu.VMEM((1024, 2 * NB), F32),
            pltpu.VMEM((2, 2 * NB, 1024), F32),
            pltpu.VMEM((2, NB, NB), F32),
            pltpu.VMEM((NB, NB), BF16),
            pltpu.VMEM((NB, NB), F32),
            pltpu.VMEM((NB, NB), F32),
            pltpu.VMEM((NB, NB), F32),
            pltpu.VMEM((NB, 3 * NB), F32),
            pltpu.VMEM((NB, 2 * NB), F32),
            pltpu.VMEM((8, 8, 128), F32),
            pltpu.VMEM((1024, NB), F32),
            pltpu.VMEM((NB, 1024), F32),
            dma((10,)),
            dma((2, 4)),
            dma((7, 4)),
            dma((7, 16)),
            dma((7, 4)),
            dma((7, 4)),
            dma((PIECES, 14)),
            dma((PIECES,)),
            dma((3,)),
            dma((3,)),
        ],
        compiler_params=pltpu.CompilerParams(
            collective_id=0, has_side_effects=True, vmem_limit_bytes=48 << 20
        ),
        name="panels",
    )(a)
    steps = 4
    rows = 1024 // steps
    out = pl.pallas_call(
        trailing_kernel,
        grid=(steps,),
        out_shape=jax.ShapeDtypeStruct((1024, 8, 128), F32),
        in_specs=[vmem] * 6,
        out_specs=pl.BlockSpec((rows, 8, 128), lambda i: (i, 0, 0)),
        compiler_params=pltpu.CompilerParams(vmem_limit_bytes=32 << 20),
        name="trailing",
    )(a, *panels)
    return out.reshape(shape)


def solution(mesh):
    spec = P(None, "row", None, None, "col", None)
    return jax.shard_map(
        on_device, mesh=mesh, in_specs=(spec,), out_specs=spec, check_vma=False
    )
```

```python
import jax
import jax.numpy as jnp
from jax import lax
from jax.experimental import pallas as pl
from jax.experimental.pallas import tpu as pltpu
from jax.sharding import PartitionSpec as P

MESH = pl.DeviceIdType.MESH
HI = lax.Precision.HIGHEST
F32 = jnp.float32
BF16 = jnp.bfloat16
NB = 256
R_PARTS = [(32, 0, 8, 0), (32, 256, 8, 0), (32, 512, 16, 8)]
C_PARTS = [(16, 0, 16, 0), (16, 256, 16, 0)]
PARTS = R_PARTS + C_PARTS + C_PARTS
HOP = 4
EARLY = 5
PIECES = 8


def pair(value):
    high = value.astype(BF16)
    return high, (value - high.astype(F32)).astype(BF16)


def product(a, b, dims):
    (high_a, low_a), (high_b, low_b) = [v if isinstance(v, tuple) else pair(v) for v in (a, b)]

    def dot(p, q):
        return lax.dot_general(p, q, dims, preferred_element_type=F32)

    return dot(high_a, high_b) + (dot(high_a, low_b) + dot(low_a, high_b))


def lane_pick(value, lane):
    return jnp.take_along_axis(value, jnp.full(value.shape, lane, jnp.int32), axis=1)


def small_inverse(v_ref, half):
    group = lax.broadcasted_iota(jnp.int32, (8, 8, 128), 0)
    sub = lax.broadcasted_iota(jnp.int32, (8, 128), 0)

    def panel(p, _):
        r = v_ref[p]
        base = 8 * p + half
        s, low, t, inv = {}, {}, {}, []
        for k in range(8):
            c = lane_pick(r, base + k)
            for i in range(k, 8):
                s[i, k] = jnp.broadcast_to(c[i : i + 1], (8, 128))
        for k in range(8):
            rk = lax.rsqrt(s[k, k])
            inv.append(rk)
            for i in range(k + 1, 8):
                low[i, k] = s[i, k] * rk
            for j in range(k + 1, 8):
                for i in range(j, 8):
                    s[i, j] = s[i, j] - low[i, k] * low[j, k]
        for i in range(8):
            t[i, i] = inv[i]
            for j in range(i):
                acc = low[i, j] * t[j, j]
                for m in range(j + 1, i):
                    acc = acc + low[i, m] * t[m, j]
                t[i, j] = -(inv[i] * acc)
        rows = [jnp.broadcast_to(r[j : j + 1], (8, 128)) for j in range(8)]
        new = []
        for k in range(8):
            acc = t[k, 0] * rows[0]
            for j in range(1, k + 1):
                acc = acc + t[k, j] * rows[j]
            new.append(acc)
        out = new[0]
        for k in range(1, 8):
            out = jnp.where(sub == k, new[k], out)
        update = None
        for j in range(8):
            z = t[7, j] * new[7]
            for k in range(j, 7):
                z = z + t[k, j] * new[k]
            c = jnp.stack([lane_pick(v_ref[g], base + j) for g in range(8)])
            term = c * z[None]
            update = term if update is None else update + term
        v = v_ref[...]
        v_ref[...] = jnp.where(group > p, v - update, jnp.where(group == p, out[None], v))
        return 0

    lax.fori_loop(0, 8, panel, 0)


def invert_block(g_ref, v_ref, q):
    lane = lax.broadcasted_iota(jnp.int32, (64, 128), 1)
    row = lax.broadcasted_iota(jnp.int32, (64, 128), 0)
    half = (q % 2) * 64
    rows = pl.ds(pl.multiple_of(64 * q, 64), 64)
    tile = pl.ds(pl.multiple_of((q // 2) * 128, 128), 128)
    mine = (lane >= half) & (lane < half + 64)
    eye = ((lane - (64 - half)) == row).astype(F32)
    v_ref[...] = jnp.where(mine, g_ref[rows, tile], eye).reshape(8, 8, 128)
    small_inverse(v_ref, half)


def factor(g_ref, v_ref, ready, after):
    lane = lax.broadcasted_iota(jnp.int32, (64, 128), 1)
    lanes = lax.broadcasted_iota(jnp.int32, (64, NB), 1)

    def block(q, _):
        half = lax.rem(q, 2) * 64
        rows = pl.ds(pl.multiple_of(64 * q, 64), 64)
        mine = (lane >= half) & (lane < half + 64)

        @pl.when(q > 0)
        def _():
            invert_block(g_ref, v_ref, q)

        ready(q)
        t = jnp.where(mine, 0.0, v_ref[...].reshape(64, 128))
        gq = g_ref[rows, :]
        u = product(t, jnp.concatenate([gq, gq], axis=0), (((1,), (0,)), ((), ())))
        g_ref[rows, :] = u
        after(q, rows, u)
        left = jnp.where(lanes >= 64 * (q + 1), u[:, :NB], 0.0)

        @pl.when(q < 3)
        def _():
            g_ref[...] -= product(left, u, (((0,), (0,)), ((), ())))

        return 0

    lax.fori_loop(0, 4, block, 0)


def every(*conditions):
    result = conditions[0]
    for condition in conditions[1:]:
        result = result & condition
    return result


def gather_kernel(
    a_ref, w0row, w1row, w0col, w1col, newcol,
    hand_r, hand_c, rraw, craw, linv, w10, low1, a01, a11, g0, g1, v_ref, r1h, r1l, c1h, c1l,
    load_sem, h_sem, t_send, t_recv, s_send, s_recv, l_send, l_recv, x_send, x_recv,
):
    row, col = lax.axis_index("row"), lax.axis_index("col")
    x, y, z, k = row // 4, row % 4, col // 2, col % 2

    def device(x, y, z, k):
        return ((x + 4) % 4 * 4 + (y + 4) % 4, (z + 8) % 8 * 2 + (k + 2) % 2)

    def shifted(offset, sign=1):
        dx, dy, dz, dk = offset
        return (
            (x + sign * dx + 4) % 4, (y + sign * dy + 4) % 4,
            (z + sign * dz + 8) % 8, (k + sign * dk + 2) % 2,
        )

    from0 = jnp.where(y == 2, 2, jnp.where(y == 0, 0, 1))
    from1 = jnp.where(y == 3, 2, jnp.where(y == 1, 0, 1))
    back = (4 - x) % 4
    trees = [
        ([((0, 0, 1, 0), lambda x, y, z, k: (k == 1) & (z != 7))], z),
        ([((0, 0, -1, 0), lambda x, y, z, k: (k == 1) & (z != 1))], (8 - z) % 8),
        (
            [
                ((0, 0, 1, 0), lambda x, y, z, k: (k == 1) & (z <= 3)),
                ((0, 0, -1, 0), lambda x, y, z, k: (k == 1) & ((z == 0) | (z >= 6))),
            ],
            jnp.where(z > 4, 8 - z, z),
        ),
        (
            [
                ((-1, 0, 0, 0), lambda x, y, z, k: (k == 1) & (y == 0) & (x != 1)),
                ((0, 1, 0, 0), lambda x, y, z, k: (k == 1) & (y == 0) & (x != 0)),
                ((0, -1, 0, 0), lambda x, y, z, k: (k == 1) & ((y == 0) | (y == 3)) & (x != 0)),
                ((1, 0, 0, 0), lambda x, y, z, k: (k == 1) & (x == 3) & (y != 0)),
            ],
            jnp.where((x == 0) & (y != 0), 2 + from0, back + from0),
        ),
        (
            [
                ((-1, 0, 0, 0), lambda x, y, z, k: (k == 1) & (y != 0) & (x != 1)),
                ((0, 1, 0, 0), lambda x, y, z, k: (k == 1) & jnp.where(x == 0, y == 0, y == 3)),
                ((0, -1, 0, 0), lambda x, y, z, k: (k == 1) & ((y == 0) | (y == 3)) & (x == 0)),
            ],
            jnp.where((x != 0) & (y == 0), 2 + back, back + from0),
        ),
        (
            [
                ((1, 0, 0, 0), lambda x, y, z, k: (k == 1) & (y == 1) & (x != 3)),
                ((0, -1, 0, 0), lambda x, y, z, k: (k == 1) & (y == 1) & (x != 0)),
                ((0, 1, 0, 0), lambda x, y, z, k: (k == 1) & ((y == 1) | (y == 2)) & (x != 0)),
                ((-1, 0, 0, 0), lambda x, y, z, k: (k == 1) & (x == 1) & (y != 1)),
            ],
            jnp.where((x == 0) & (y != 1), 2 + from1, x + from1),
        ),
        (
            [
                ((1, 0, 0, 0), lambda x, y, z, k: (k == 1) & (y != 1) & (x != 3)),
                ((0, -1, 0, 0), lambda x, y, z, k: (k == 1) & jnp.where(x == 0, y == 1, y == 2)),
                ((0, 1, 0, 0), lambda x, y, z, k: (k == 1) & ((y == 1) | (y == 2)) & (x == 0)),
            ],
            jnp.where((x != 0) & (y == 1), 2 + x, x + from1),
        ),
    ]

    def branch(y, k):
        return (y == 0) & (k == 0)

    def entry(z):
        return jnp.where(z == 4, 2, jnp.where((z == 2) | (z == 6), 1, jnp.where((z == 3) | (z == 5), 3, 0)))

    def along_z(at):
        return lambda x, y, z, k: branch(y, k) & (z == 0) & (x == at)

    def along_x(x, y, z, k):
        return branch(y, k) & (x == entry(z))

    def along_y(x, y, z, k):
        return branch(y, k)

    l_edges = [
        ((1, 0, 0, 0), lambda x, y, z, k: branch(y, k) & ((x == entry(z)) | (x == (entry(z) + 1) % 4))),
        ((-1, 0, 0, 0), along_x),
        ((0, 0, 1, 0), along_z(0)),
        ((0, 0, -1, 0), along_z(0)),
        ((0, 0, 2, 0), along_z(1)),
        ((0, 0, -2, 0), along_z(1)),
        ((0, 0, 4, 0), along_z(2)),
        ((0, 0, 3, 0), along_z(3)),
        ((0, 0, -3, 0), along_z(3)),
        ((0, -1, 0, 0), lambda x, y, z, k: (y == 3) & (k == 0)),
        ((0, 2, 0, 0), along_y),
        ((0, 1, 0, 0), along_y),
        ((0, -1, 0, 0), along_y),
        ((0, 0, 0, 1), lambda x, y, z, k: k == 0),
    ]
    early_edge, late_edge = 9, 10
    corner = every(row == 0, col == 0)
    beside = every(row == 0, col == 1)
    below = every(row == 1, col == 1)
    first, second = k == 0, k == 1
    r_source = z == 0
    c_source = [every(x == 0, y == 0), every(x == 0, y == 1)]
    root = [r_source, r_source, r_source, c_source[0], c_source[0], c_source[1], c_source[1]]

    def r_load(t, dst, lane):
        return pltpu.make_async_copy(
            a_ref.at[:, t, :], dst.at[:, pl.ds(lane + 128 * t, 128)], load_sem.at[t]
        )

    def c_load(t, dst):
        return pltpu.make_async_copy(
            a_ref.at[pl.ds(0, NB), t, :], dst.at[:, pl.ds(128 * t, 128)], load_sem.at[2 + t]
        )

    own = pl.ds(pl.multiple_of(NB * k, NB), NB)

    def c_loads(act, some):
        for s in range(2):
            @pl.when(c_source[s] & first)
            def _():
                for t in some:
                    act(c_load(t, hand_c))

            @pl.when(c_source[s] & second)
            def _():
                for t in some:
                    act(c_load(t, craw.at[s, pl.ds(NB, NB)]))

    def r_loads(act):
        @pl.when(r_source)
        def _():
            for t in range(2):
                act(r_load(t, hand_r, 0))

    c_loads(lambda copy: copy.start(), range(8))
    r_loads(lambda copy: copy.start())

    barrier = pltpu.get_barrier_semaphore()

    def greet(target):
        pl.semaphore_signal(barrier, inc=1, device_id=device(*target), device_id_type=MESH)

    awaited = jnp.where(beside, 2, 1) + jnp.where(below, 1, 0) + jnp.where(corner, 1, 0)
    greet((x, y, z, 1 - k))
    for offset, sends in [edge for edges, _ in trees for edge in edges] + l_edges[:-1]:
        awaited = awaited + sends(x, y, z, k).astype(jnp.int32)
        parent = shifted(offset, -1)

        @pl.when(sends(*parent))
        def _():
            greet(parent)

    @pl.when(corner)
    def _():
        greet((0, 0, 0, 1))
        greet((0, 1, 0, 1))

    @pl.when(below)
    def _():
        greet((0, 0, 0, 0))

    linv[0, pl.ds(0, 128), pl.ds(128, 128)] = jnp.zeros((128, 128), F32)
    linv[1, pl.ds(0, 128), pl.ds(128, 128)] = jnp.zeros((128, 128), F32)
    c_loads(lambda copy: copy.wait(), range(2))

    @pl.when(corner)
    def _():
        eye = (
            lax.broadcasted_iota(jnp.int32, (NB, NB), 0) == lax.broadcasted_iota(jnp.int32, (NB, NB), 1)
        ).astype(F32)
        g0[:, :NB] = hand_c[:, :NB]
        g0[:, 2 * NB :] = eye
        g1[:, :NB] = jnp.zeros((NB, NB), F32)
        g1[:, NB:] = eye
        invert_block(g0, v_ref, 0)

    pl.semaphore_wait(barrier, awaited)

    def remote(src, dst, send, recv, target):
        return pltpu.make_async_remote_copy(
            src_ref=src, dst_ref=dst, send_sem=send, recv_sem=recv,
            device_id=target, device_id_type=MESH,
        )

    t_on = [[sends(x, y, z, k) for _, sends in edges] for edges, _ in trees]
    t_to = [[device(*shifted(offset)) for offset, _ in edges] for edges, _ in trees]
    l_on = [sends(x, y, z, k) for _, sends in l_edges]
    l_to = [device(*shifted(offset)) for offset, _ in l_edges]
    sibling = device(x, y, z, 1 - k)
    first_step = [PARTS[u][3] + HOP * depth for u, (_, depth) in enumerate(trees)]

    def t_ref(u, start, count):
        rows, top, _, _ = PARTS[u]
        span = pl.ds(pl.multiple_of(top + rows * start, rows), rows * count)
        return rraw.at[span, :] if u < 3 else craw.at[(u - 3) // 2, span, :]

    def t_copy(u, n, e=0):
        part = t_ref(u, 0, PARTS[u][2]) if n is None else t_ref(u, n, 1)
        return remote(part, part, t_send.at[u, e], t_recv.at[u, 0 if n is None else n], t_to[u][e])

    def s_copy(u, i):
        part = t_ref(u, 4 * i, 4)
        return remote(part, part, s_send.at[u, i], s_recv.at[u, i], sibling)

    for_first = (0, 1, 2, 3, 5)

    def h_copy(i):
        if i < 2:
            src, dst = hand_r.at[pl.ds(512 * i, 512), :], rraw.at[pl.ds(512 * i, 512), pl.ds(0, NB)]
        else:
            half = pl.ds(128 * (i - 2), 128)
            src, dst = hand_c.at[half, :], craw.at[row % 2, half, :]
        return remote(src, dst, h_sem.at[0, i], h_sem.at[1, i], sibling)

    pieces = [
        linv.at[0, pl.ds(0, 128), pl.ds(0, 128)],
        w10.at[pl.ds(0, 128), :],
        linv.at[0, pl.ds(128, 64), :],
        linv.at[0, pl.ds(192, 64), :],
        w10.at[pl.ds(128, 128), :],
        linv.at[1, pl.ds(0, 128), pl.ds(0, 128)],
        linv.at[1, pl.ds(128, 64), :],
        linv.at[1, pl.ds(192, 64), :],
    ]

    def l_copy(p, e):
        return remote(pieces[p], pieces[p], l_send.at[p, e], l_recv.at[p], l_to[e])

    def edges_of(p):
        skipped = late_edge if p < EARLY else early_edge
        return [(e, on) for e, on in enumerate(l_on) if e != skipped]

    def send_piece(p):
        for e, on in edges_of(p):
            @pl.when(on)
            def _():
                l_copy(p, e).start()

    def wait_pieces(some):
        for p in some:
            l_copy(p, 0).wait_recv()

    def pass_pieces(some):
        for p in some:
            l_copy(p, 0).wait_recv()
            send_piece(p)

    def a01_copy():
        return remote(craw.at[0, pl.ds(NB, NB), pl.ds(0, NB)], a01, x_send.at[0], x_recv.at[0], (0, 0))

    def a11_copy():
        return remote(craw.at[1, pl.ds(NB, NB), pl.ds(0, NB)], a11, x_send.at[1], x_recv.at[1], (0, 0))

    def low1_copy():
        return remote(low1, low1, x_send.at[2], x_recv.at[2], (1, 1))

    @pl.when(beside)
    def _():
        a01_copy().start()

    @pl.when(below)
    def _():
        a11_copy().start()

    c_root = c_source[0] | c_source[1]
    halves = [r_source, r_source, c_root, c_root]

    def hand_over():
        c_loads(lambda copy: copy.wait(), range(2, 8))
        r_loads(lambda copy: copy.wait())
        for i in (0, 2, 1, 3):
            @pl.when(halves[i] & first)
            def _():
                h_copy(i).start()

    hand_over()

    @pl.when(r_source & second)
    def _():
        rraw[:, NB:] = hand_r[...]

    @pl.when(corner)
    def _():
        def ready0(q):
            @pl.when(q == 0)
            def _():
                a01_copy().wait_recv()
                g0[:, NB : 2 * NB] = a01[...]

        def after0(q, rows, u):
            linv[0, rows, :] = u[:, 2 * NB :]
            w = u[:, NB : 2 * NB].astype(BF16)
            w10[rows, :] = w
            g1[:, :NB] -= lax.dot_general(w, w, (((0,), (0,)), ((), ())), preferred_element_type=F32)

            @pl.when(q == 1)
            def _():
                send_piece(0)
                send_piece(1)

            @pl.when(q == 2)
            def _():
                send_piece(2)

            @pl.when(q == 3)
            def _():
                send_piece(3)
                send_piece(4)

        factor(g0, v_ref, ready0, after0)
        a11_copy().wait_recv()
        g1[:, :NB] += a11[...]
        invert_block(g1, v_ref, 0)

        def after1(q, rows, u):
            linv[1, rows, :] = u[:, NB:]
            low1[rows, :] = u[:, :NB]
            for i in range(3):
                @pl.when(q == i + 1)
                def _():
                    send_piece(EARLY + i)

        factor(g1, v_ref, lambda q: None, after1)
        low1_copy().start()

    @pl.when(first & jnp.logical_not(corner))
    def _():
        pass_pieces(range(EARLY))

    @pl.when(branch(y, k) & jnp.logical_not(corner))
    def _():
        pass_pieces(range(EARLY, PIECES))

    @pl.when(second)
    def _():
        def step(m, _):
            for i in range(4):
                @pl.when(halves[i] & (m == 8 * (i % 2)))
                def _():
                    h_copy(i).wait_recv()

            for u in range(7):
                n = m - first_step[u]

                @pl.when((n >= 0) & (n < PARTS[u][2]))
                def _():
                    @pl.when(jnp.logical_not(root[u]))
                    def _():
                        t_copy(u, n).wait_recv()

                    for e, on in enumerate(t_on[u]):
                        @pl.when(on)
                        def _():
                            t_copy(u, n, e).start()

                    if u in for_first:
                        @pl.when(n % 4 == 3)
                        def _():
                            s_copy(u, n // 4).start()

            return 0

        lax.fori_loop(0, 40, step, 0)
        wait_pieces(range(EARLY))

    def wait_parts(u, some):
        @pl.when(first)
        def _():
            for i in some:
                s_copy(u, i).wait_recv()

    inverse = pair(linv[0])
    upper = lax.broadcasted_iota(jnp.int32, (NB, NB), 1) > lax.broadcasted_iota(jnp.int32, (NB, NB), 0)
    nn = (((1,), (0,)), ((), ()))
    nt = (((1,), (1,)), ((), ()))
    tn = (((0,), (0,)), ((), ()))
    for b in range(4):
        rows = pl.ds(NB * b, NB)
        wait_parts(min(b, 2), range(2 * (b // 3), 2 + 2 * (b // 3)))
        solved = product(rraw[rows, pl.ds(0, NB)], inverse, nt)
        newcol[rows, :] = solved
        rounded = solved.astype(BF16)
        if b == 0:
            rounded = jnp.where(row == 0, jnp.zeros_like(rounded), rounded)
        w0row[rows, :] = rounded
        r1h[rows, :], r1l[rows, :] = pair(
            rraw[rows, pl.ds(NB, NB)] - jnp.dot(rounded, w10[...], preferred_element_type=F32)
        )
    wait_parts(3, range(4))
    wait_parts(5, range(4))
    for b in range(4):
        rows = pl.ds(NB * b, NB)
        solved = product(inverse, craw[0, own, rows], nn)
        rounded = solved.astype(BF16)
        if b == 0:
            rounded = jnp.where(col == 0, jnp.zeros_like(rounded), rounded)
        w0col[:, rows] = rounded
        c1h[:, rows], c1l[:, rows] = pair(
            craw[1, own, rows] - lax.dot_general(w10[...], rounded, tn, preferred_element_type=F32)
        )

    def drain_pieces(some):
        for p in some:
            for e, on in edges_of(p):
                @pl.when(on)
                def _():
                    l_copy(p, e).wait_send()

    for u in range(7):
        for e, on in enumerate(t_on[u]):
            @pl.when(on)
            def _():
                t_copy(u, None, e).wait_send()

    @pl.when(second)
    def _():
        for u in for_first:
            for i in range(PARTS[u][2] // 4):
                s_copy(u, i).wait_send()

    for i in range(4):
        @pl.when(halves[i] & first)
        def _():
            h_copy(i).wait_send()

    @pl.when(beside)
    def _():
        a01_copy().wait_send()

    @pl.when(below)
    def _():
        a11_copy().wait_send()

    drain_pieces(range(EARLY))

    @pl.when(first & (y != 0))
    def _():
        pass_pieces(range(EARLY, PIECES))

    @pl.when(second)
    def _():
        wait_pieces(range(EARLY, PIECES))

    inverse = pair(linv[1])
    for b in range(4):
        rows = pl.ds(NB * b, NB)
        solved = product((r1h[rows, :], r1l[rows, :]), inverse, nt)
        rounded = solved.astype(BF16)
        if b == 0:
            rounded = jnp.where(row <= 1, jnp.zeros_like(rounded), rounded)
            solved = jnp.where(row == 0, rraw[rows, pl.ds(NB, NB)], solved)
        w1row[rows, :] = rounded

        @pl.when(col == 1)
        def _():
            newcol[rows, :] = solved

        solved = product(inverse, (c1h[:, rows], c1l[:, rows]), nn)
        rounded = solved.astype(BF16)
        if b == 0:
            rounded = jnp.where(col <= 1, jnp.zeros_like(rounded), rounded)
        w1col[:, rows] = rounded

    @pl.when(corner)
    def _():
        newcol[pl.ds(0, NB), :] = jnp.where(upper, 0.0, g0[:, :NB].T)

    @pl.when(below)
    def _():
        low1_copy().wait_recv()
        newcol[pl.ds(0, NB), :] = jnp.where(upper, 0.0, low1[...].T)

    drain_pieces(range(EARLY, PIECES))

    @pl.when(corner)
    def _():
        low1_copy().wait_send()


def trailing_kernel(a_ref, w0row, w1row, w0col, w1col, newcol, o_ref):
    count = o_ref.shape[0]
    rows = pl.ds(pl.multiple_of(pl.program_id(0) * count, count), count)
    update = jnp.dot(w0row[rows, :], w0col[...], preferred_element_type=F32)
    update += jnp.dot(w1row[rows, :], w1col[...], preferred_element_type=F32)
    o_ref[...] = a_ref[rows] - update.reshape(count, 8, 128)

    @pl.when(lax.axis_index("col") <= 1)
    def _():
        for t in range(2):
            o_ref[:, t, :] = newcol[rows, pl.ds(128 * t, 128)]


def on_device(covariance):
    shape = covariance.shape
    a = covariance.reshape(1024, 8, 128)
    vmem = pl.BlockSpec(memory_space=pltpu.VMEM)
    dma = pltpu.SemaphoreType.DMA
    panels = pl.pallas_call(
        gather_kernel,
        out_shape=(
            jax.ShapeDtypeStruct((1024, NB), BF16),
            jax.ShapeDtypeStruct((1024, NB), BF16),
            jax.ShapeDtypeStruct((NB, 1024), BF16),
            jax.ShapeDtypeStruct((NB, 1024), BF16),
            jax.ShapeDtypeStruct((1024, NB), F32),
        ),
        in_specs=[pl.BlockSpec(memory_space=pl.ANY)],
        out_specs=(vmem,) * 5,
        scratch_shapes=[
            pltpu.VMEM((1024, NB), F32),
            pltpu.VMEM((NB, 1024), F32),
            pltpu.VMEM((1024, 2 * NB), F32),
            pltpu.VMEM((2, 2 * NB, 1024), F32),
            pltpu.VMEM((2, NB, NB), F32),
            pltpu.VMEM((NB, NB), BF16),
            pltpu.VMEM((NB, NB), F32),
            pltpu.VMEM((NB, NB), F32),
            pltpu.VMEM((NB, NB), F32),
            pltpu.VMEM((NB, 3 * NB), F32),
            pltpu.VMEM((NB, 2 * NB), F32),
            pltpu.VMEM((8, 8, 128), F32),
            pltpu.VMEM((1024, NB), BF16),
            pltpu.VMEM((1024, NB), BF16),
            pltpu.VMEM((NB, 1024), BF16),
            pltpu.VMEM((NB, 1024), BF16),
            dma((10,)),
            dma((2, 4)),
            dma((7, 4)),
            dma((7, 16)),
            dma((7, 4)),
            dma((7, 4)),
            dma((PIECES, 14)),
            dma((PIECES,)),
            dma((3,)),
            dma((3,)),
        ],
        compiler_params=pltpu.CompilerParams(
            collective_id=0, has_side_effects=True, vmem_limit_bytes=48 << 20
        ),
        name="panels",
    )(a)
    steps = 4
    rows = 1024 // steps
    out = pl.pallas_call(
        trailing_kernel,
        grid=(steps,),
        out_shape=jax.ShapeDtypeStruct((1024, 8, 128), F32),
        in_specs=[vmem] * 6,
        out_specs=pl.BlockSpec((rows, 8, 128), lambda i: (i, 0, 0)),
        compiler_params=pltpu.CompilerParams(vmem_limit_bytes=32 << 20),
        name="trailing",
    )(a, *panels)
    return out.reshape(shape)


def solution(mesh):
    spec = P(None, "row", None, None, "col", None)
    return jax.shard_map(
        on_device, mesh=mesh, in_specs=(spec,), out_specs=spec, check_vma=False
    )
```

```python
import jax
import jax.numpy as jnp
from jax import lax
from jax.experimental import pallas as pl
from jax.experimental.pallas import tpu as pltpu
from jax.sharding import PartitionSpec as P

MESH = pl.DeviceIdType.MESH
HI = lax.Precision.HIGHEST
F32 = jnp.float32
BF16 = jnp.bfloat16
NB = 256
R_PARTS = [(32, 0, 8, 0), (32, 256, 8, 0), (32, 512, 16, 8)]
C_PARTS = [(16, 0, 16, 0), (16, 256, 16, 0)]
PARTS = R_PARTS + C_PARTS + C_PARTS
HOP = 4
EARLY = 5
PIECES = 8


def pair(value):
    high = value.astype(BF16)
    return high, (value - high.astype(F32)).astype(BF16)


def product(a, b, dims):
    (high_a, low_a), (high_b, low_b) = [v if isinstance(v, tuple) else pair(v) for v in (a, b)]

    def dot(p, q):
        return lax.dot_general(p, q, dims, preferred_element_type=F32)

    return dot(high_a, high_b) + (dot(high_a, low_b) + dot(low_a, high_b))


def lane_pick(value, lane):
    return jnp.take_along_axis(value, jnp.full(value.shape, lane, jnp.int32), axis=1)


def small_inverse(v_ref, half):
    group = lax.broadcasted_iota(jnp.int32, (8, 8, 128), 0)
    sub = lax.broadcasted_iota(jnp.int32, (8, 128), 0)

    def panel(p, _):
        r = v_ref[p]
        base = 8 * p + half
        s, low, t, inv = {}, {}, {}, []
        for k in range(8):
            c = lane_pick(r, base + k)
            for i in range(k, 8):
                s[i, k] = jnp.broadcast_to(c[i : i + 1], (8, 128))
        for k in range(8):
            rk = lax.rsqrt(s[k, k])
            inv.append(rk)
            for i in range(k + 1, 8):
                low[i, k] = s[i, k] * rk
            for j in range(k + 1, 8):
                for i in range(j, 8):
                    s[i, j] = s[i, j] - low[i, k] * low[j, k]
        for i in range(8):
            t[i, i] = inv[i]
            for j in range(i):
                acc = low[i, j] * t[j, j]
                for m in range(j + 1, i):
                    acc = acc + low[i, m] * t[m, j]
                t[i, j] = -(inv[i] * acc)
        rows = [jnp.broadcast_to(r[j : j + 1], (8, 128)) for j in range(8)]
        new = []
        for k in range(8):
            acc = t[k, 0] * rows[0]
            for j in range(1, k + 1):
                acc = acc + t[k, j] * rows[j]
            new.append(acc)
        out = new[0]
        for k in range(1, 8):
            out = jnp.where(sub == k, new[k], out)
        update = None
        for j in range(8):
            z = t[7, j] * new[7]
            for k in range(j, 7):
                z = z + t[k, j] * new[k]
            c = jnp.stack([lane_pick(v_ref[g], base + j) for g in range(8)])
            term = c * z[None]
            update = term if update is None else update + term
        v = v_ref[...]
        v_ref[...] = jnp.where(group > p, v - update, jnp.where(group == p, out[None], v))
        return 0

    lax.fori_loop(0, 8, panel, 0)


def invert_block(g_ref, v_ref, q):
    lane = lax.broadcasted_iota(jnp.int32, (64, 128), 1)
    row = lax.broadcasted_iota(jnp.int32, (64, 128), 0)
    half = (q % 2) * 64
    rows = pl.ds(pl.multiple_of(64 * q, 64), 64)
    tile = pl.ds(pl.multiple_of((q // 2) * 128, 128), 128)
    mine = (lane >= half) & (lane < half + 64)
    eye = ((lane - (64 - half)) == row).astype(F32)
    v_ref[...] = jnp.where(mine, g_ref[rows, tile], eye).reshape(8, 8, 128)
    small_inverse(v_ref, half)


def factor(g_ref, v_ref, ready, after):
    lane = lax.broadcasted_iota(jnp.int32, (64, 128), 1)
    lanes = lax.broadcasted_iota(jnp.int32, (64, NB), 1)

    def block(q, _):
        half = lax.rem(q, 2) * 64
        rows = pl.ds(pl.multiple_of(64 * q, 64), 64)
        mine = (lane >= half) & (lane < half + 64)

        @pl.when(q > 0)
        def _():
            invert_block(g_ref, v_ref, q)

        ready(q)
        t = jnp.where(mine, 0.0, v_ref[...].reshape(64, 128))
        gq = g_ref[rows, :]
        u = product(t, jnp.concatenate([gq, gq], axis=0), (((1,), (0,)), ((), ())))
        g_ref[rows, :] = u
        after(q, rows, u)
        left = jnp.where(lanes >= 64 * (q + 1), u[:, :NB], 0.0)

        @pl.when(q < 3)
        def _():
            g_ref[...] -= product(left, u, (((0,), (0,)), ((), ())))

        return 0

    lax.fori_loop(0, 4, block, 0)


def every(*conditions):
    result = conditions[0]
    for condition in conditions[1:]:
        result = result & condition
    return result


def gather_kernel(
    a_ref, w0row, w1row, w0col, w1col, newcol,
    hand_r, hand_c, rraw, craw, linv, w10, low1, a01, a11, g0, g1, v_ref, r1h, r1l, c1h, c1l,
    load_sem, h_sem, t_send, t_recv, s_send, s_recv, l_send, l_recv, x_send, x_recv,
):
    row, col = lax.axis_index("row"), lax.axis_index("col")
    x, y, z, k = row // 4, row % 4, col // 2, col % 2

    def device(x, y, z, k):
        return ((x + 4) % 4 * 4 + (y + 4) % 4, (z + 8) % 8 * 2 + (k + 2) % 2)

    def shifted(offset, sign=1):
        dx, dy, dz, dk = offset
        return (
            (x + sign * dx + 4) % 4, (y + sign * dy + 4) % 4,
            (z + sign * dz + 8) % 8, (k + sign * dk + 2) % 2,
        )

    from0 = jnp.where(y == 2, 2, jnp.where(y == 0, 0, 1))
    from1 = jnp.where(y == 3, 2, jnp.where(y == 1, 0, 1))
    back = (4 - x) % 4
    trees = [
        ([((0, 0, 1, 0), lambda x, y, z, k: (k == 1) & (z != 7))], z),
        ([((0, 0, -1, 0), lambda x, y, z, k: (k == 1) & (z != 1))], (8 - z) % 8),
        (
            [
                ((0, 0, 1, 0), lambda x, y, z, k: (k == 1) & (z <= 3)),
                ((0, 0, -1, 0), lambda x, y, z, k: (k == 1) & ((z == 0) | (z >= 6))),
            ],
            jnp.where(z > 4, 8 - z, z),
        ),
        (
            [
                ((-1, 0, 0, 0), lambda x, y, z, k: (k == 1) & (y == 0) & (x != 1)),
                ((0, 1, 0, 0), lambda x, y, z, k: (k == 1) & (y == 0) & (x != 0)),
                ((0, -1, 0, 0), lambda x, y, z, k: (k == 1) & ((y == 0) | (y == 3)) & (x != 0)),
                ((1, 0, 0, 0), lambda x, y, z, k: (k == 1) & (x == 3) & (y != 0)),
            ],
            jnp.where((x == 0) & (y != 0), 2 + from0, back + from0),
        ),
        (
            [
                ((-1, 0, 0, 0), lambda x, y, z, k: (k == 1) & (y != 0) & (x != 1)),
                ((0, 1, 0, 0), lambda x, y, z, k: (k == 1) & jnp.where(x == 0, y == 0, y == 3)),
                ((0, -1, 0, 0), lambda x, y, z, k: (k == 1) & ((y == 0) | (y == 3)) & (x == 0)),
            ],
            jnp.where((x != 0) & (y == 0), 2 + back, back + from0),
        ),
        (
            [
                ((1, 0, 0, 0), lambda x, y, z, k: (k == 1) & (y == 1) & (x != 3)),
                ((0, -1, 0, 0), lambda x, y, z, k: (k == 1) & (y == 1) & (x != 0)),
                ((0, 1, 0, 0), lambda x, y, z, k: (k == 1) & ((y == 1) | (y == 2)) & (x != 0)),
                ((-1, 0, 0, 0), lambda x, y, z, k: (k == 1) & (x == 1) & (y != 1)),
            ],
            jnp.where((x == 0) & (y != 1), 2 + from1, x + from1),
        ),
        (
            [
                ((1, 0, 0, 0), lambda x, y, z, k: (k == 1) & (y != 1) & (x != 3)),
                ((0, -1, 0, 0), lambda x, y, z, k: (k == 1) & jnp.where(x == 0, y == 1, y == 2)),
                ((0, 1, 0, 0), lambda x, y, z, k: (k == 1) & ((y == 1) | (y == 2)) & (x == 0)),
            ],
            jnp.where((x != 0) & (y == 1), 2 + x, x + from1),
        ),
    ]

    def branch(y, k):
        return (y == 0) & (k == 0)

    def entry(z):
        return jnp.where(z == 4, 2, jnp.where((z == 2) | (z == 6), 1, jnp.where((z == 3) | (z == 5), 3, 0)))

    def along_z(at):
        return lambda x, y, z, k: branch(y, k) & (z == 0) & (x == at)

    def along_x(x, y, z, k):
        return branch(y, k) & (x == entry(z))

    def along_y(x, y, z, k):
        return branch(y, k)

    l_edges = [
        ((1, 0, 0, 0), lambda x, y, z, k: branch(y, k) & ((x == entry(z)) | (x == (entry(z) + 1) % 4))),
        ((-1, 0, 0, 0), along_x),
        ((0, 0, 1, 0), along_z(0)),
        ((0, 0, -1, 0), along_z(0)),
        ((0, 0, 2, 0), along_z(1)),
        ((0, 0, -2, 0), along_z(1)),
        ((0, 0, 4, 0), along_z(2)),
        ((0, 0, 3, 0), along_z(3)),
        ((0, 0, -3, 0), along_z(3)),
        ((0, -1, 0, 0), lambda x, y, z, k: (y == 3) & (k == 0)),
        ((0, 2, 0, 0), along_y),
        ((0, 1, 0, 0), along_y),
        ((0, -1, 0, 0), along_y),
        ((0, 0, 0, 1), lambda x, y, z, k: k == 0),
    ]
    early_edge, late_edge = 9, 10
    corner = every(row == 0, col == 0)
    beside = every(row == 0, col == 1)
    below = every(row == 1, col == 1)
    first, second = k == 0, k == 1
    r_source = z == 0
    c_source = [every(x == 0, y == 0), every(x == 0, y == 1)]
    root = [r_source, r_source, r_source, c_source[0], c_source[0], c_source[1], c_source[1]]

    def r_load(t, dst, lane):
        return pltpu.make_async_copy(
            a_ref.at[:, t, :], dst.at[:, pl.ds(lane + 128 * t, 128)], load_sem.at[t]
        )

    def c_load(t, dst):
        return pltpu.make_async_copy(
            a_ref.at[pl.ds(0, NB), t, :], dst.at[:, pl.ds(128 * t, 128)], load_sem.at[2 + t]
        )

    own = pl.ds(pl.multiple_of(NB * k, NB), NB)

    def c_loads(act, some):
        for s in range(2):
            @pl.when(c_source[s] & first)
            def _():
                for t in some:
                    act(c_load(t, hand_c))

            @pl.when(c_source[s] & second)
            def _():
                for t in some:
                    act(c_load(t, craw.at[s, pl.ds(NB, NB)]))

    def r_loads(act):
        @pl.when(r_source)
        def _():
            for t in range(2):
                act(r_load(t, hand_r, 0))

    c_loads(lambda copy: copy.start(), range(8))
    r_loads(lambda copy: copy.start())

    barrier = pltpu.get_barrier_semaphore()

    def greet(target):
        pl.semaphore_signal(barrier, inc=1, device_id=device(*target), device_id_type=MESH)

    awaited = jnp.where(beside, 2, 1) + jnp.where(below, 1, 0) + jnp.where(corner, 1, 0)
    greet((x, y, z, 1 - k))
    for offset, sends in [edge for edges, _ in trees for edge in edges] + l_edges[:-1]:
        awaited = awaited + sends(x, y, z, k).astype(jnp.int32)
        parent = shifted(offset, -1)

        @pl.when(sends(*parent))
        def _():
            greet(parent)

    @pl.when(corner)
    def _():
        greet((0, 0, 0, 1))
        greet((0, 1, 0, 1))

    @pl.when(below)
    def _():
        greet((0, 0, 0, 0))

    linv[0, pl.ds(0, 128), pl.ds(128, 128)] = jnp.zeros((128, 128), F32)
    linv[1, pl.ds(0, 128), pl.ds(128, 128)] = jnp.zeros((128, 128), F32)
    c_loads(lambda copy: copy.wait(), range(2))

    @pl.when(corner)
    def _():
        eye = (
            lax.broadcasted_iota(jnp.int32, (NB, NB), 0) == lax.broadcasted_iota(jnp.int32, (NB, NB), 1)
        ).astype(F32)
        g0[:, :NB] = hand_c[:, :NB]
        g0[:, 2 * NB :] = eye
        g1[:, :NB] = jnp.zeros((NB, NB), F32)
        g1[:, NB:] = eye
        invert_block(g0, v_ref, 0)

    pl.semaphore_wait(barrier, awaited)

    def remote(src, dst, send, recv, target):
        return pltpu.make_async_remote_copy(
            src_ref=src, dst_ref=dst, send_sem=send, recv_sem=recv,
            device_id=target, device_id_type=MESH,
        )

    t_on = [[sends(x, y, z, k) for _, sends in edges] for edges, _ in trees]
    t_to = [[device(*shifted(offset)) for offset, _ in edges] for edges, _ in trees]
    l_on = [sends(x, y, z, k) for _, sends in l_edges]
    l_to = [device(*shifted(offset)) for offset, _ in l_edges]
    sibling = device(x, y, z, 1 - k)
    first_step = [PARTS[u][3] + HOP * depth for u, (_, depth) in enumerate(trees)]

    def t_ref(u, start, count):
        rows, top, _, _ = PARTS[u]
        span = pl.ds(pl.multiple_of(top + rows * start, rows), rows * count)
        return rraw.at[span, :] if u < 3 else craw.at[(u - 3) // 2, span, :]

    def t_copy(u, n, e=0):
        part = t_ref(u, 0, PARTS[u][2]) if n is None else t_ref(u, n, 1)
        return remote(part, part, t_send.at[u, e], t_recv.at[u, 0 if n is None else n], t_to[u][e])

    def s_copy(u, i):
        part = t_ref(u, 4 * i, 4)
        return remote(part, part, s_send.at[u, i], s_recv.at[u, i], sibling)

    for_first = (0, 1, 2, 3, 5)

    def h_copy(i):
        if i < 2:
            src, dst = hand_r.at[pl.ds(512 * i, 512), :], rraw.at[pl.ds(512 * i, 512), pl.ds(0, NB)]
        else:
            half = pl.ds(128 * (i - 2), 128)
            src, dst = hand_c.at[half, :], craw.at[row % 2, half, :]
        return remote(src, dst, h_sem.at[0, i], h_sem.at[1, i], sibling)

    pieces = [
        linv.at[0, pl.ds(0, 128), pl.ds(0, 128)],
        w10.at[pl.ds(0, 128), :],
        linv.at[0, pl.ds(128, 64), :],
        linv.at[0, pl.ds(192, 64), :],
        w10.at[pl.ds(128, 128), :],
        linv.at[1, pl.ds(0, 128), pl.ds(0, 128)],
        linv.at[1, pl.ds(128, 64), :],
        linv.at[1, pl.ds(192, 64), :],
    ]

    def l_copy(p, e):
        return remote(pieces[p], pieces[p], l_send.at[p, e], l_recv.at[p], l_to[e])

    def edges_of(p):
        skipped = late_edge if p < EARLY else early_edge
        return [(e, on) for e, on in enumerate(l_on) if e != skipped]

    def send_piece(p):
        for e, on in edges_of(p):
            @pl.when(on)
            def _():
                l_copy(p, e).start()

    def wait_pieces(some):
        for p in some:
            l_copy(p, 0).wait_recv()

    def pass_pieces(some):
        for p in some:
            l_copy(p, 0).wait_recv()
            send_piece(p)

    def a01_copy():
        return remote(craw.at[0, pl.ds(NB, NB), pl.ds(0, NB)], a01, x_send.at[0], x_recv.at[0], (0, 0))

    def a11_copy():
        return remote(craw.at[1, pl.ds(NB, NB), pl.ds(0, NB)], a11, x_send.at[1], x_recv.at[1], (0, 0))

    def low1_copy():
        return remote(low1, low1, x_send.at[2], x_recv.at[2], (1, 1))

    @pl.when(beside)
    def _():
        a01_copy().start()

    @pl.when(below)
    def _():
        a11_copy().start()

    c_root = c_source[0] | c_source[1]
    halves = [r_source, r_source, c_root, c_root]

    def hand_over():
        c_loads(lambda copy: copy.wait(), range(2, 8))
        r_loads(lambda copy: copy.wait())
        for i in (0, 2, 1, 3):
            @pl.when(halves[i] & first)
            def _():
                h_copy(i).start()

    hand_over()

    @pl.when(r_source & second)
    def _():
        rraw[:, NB:] = hand_r[...]

    @pl.when(corner)
    def _():
        def ready0(q):
            @pl.when(q == 0)
            def _():
                a01_copy().wait_recv()
                g0[:, NB : 2 * NB] = a01[...]

        def after0(q, rows, u):
            linv[0, rows, :] = u[:, 2 * NB :]
            w = u[:, NB : 2 * NB].astype(BF16)
            w10[rows, :] = w
            g1[:, :NB] -= lax.dot_general(w, w, (((0,), (0,)), ((), ())), preferred_element_type=F32)

            @pl.when(q == 1)
            def _():
                send_piece(0)
                send_piece(1)

            @pl.when(q == 2)
            def _():
                send_piece(2)

            @pl.when(q == 3)
            def _():
                send_piece(3)
                send_piece(4)

        factor(g0, v_ref, ready0, after0)
        a11_copy().wait_recv()
        g1[:, :NB] += a11[...]
        invert_block(g1, v_ref, 0)

        def after1(q, rows, u):
            linv[1, rows, :] = u[:, NB:]
            low1[rows, :] = u[:, :NB]
            for i in range(3):
                @pl.when(q == i + 1)
                def _():
                    send_piece(EARLY + i)

        factor(g1, v_ref, lambda q: None, after1)
        low1_copy().start()

    @pl.when(first & jnp.logical_not(corner))
    def _():
        pass_pieces(range(EARLY))

    @pl.when(branch(y, k) & jnp.logical_not(corner))
    def _():
        pass_pieces(range(EARLY, PIECES))

    @pl.when(second)
    def _():
        def step(m, _):
            for i in range(4):
                @pl.when(halves[i] & (m == 8 * (i % 2)))
                def _():
                    h_copy(i).wait_recv()

            for u in range(7):
                n = m - first_step[u]

                @pl.when((n >= 0) & (n < PARTS[u][2]))
                def _():
                    @pl.when(jnp.logical_not(root[u]))
                    def _():
                        t_copy(u, n).wait_recv()

                    for e, on in enumerate(t_on[u]):
                        @pl.when(on)
                        def _():
                            t_copy(u, n, e).start()

                    if u in for_first:
                        @pl.when(n % 4 == 3)
                        def _():
                            s_copy(u, n // 4).start()

            return 0

        lax.fori_loop(0, 40, step, 0)
        wait_pieces(range(EARLY))

    def wait_parts(u, some):
        @pl.when(first)
        def _():
            for i in some:
                s_copy(u, i).wait_recv()

    inverse = pair(linv[0])
    upper = lax.broadcasted_iota(jnp.int32, (NB, NB), 1) > lax.broadcasted_iota(jnp.int32, (NB, NB), 0)
    nn = (((1,), (0,)), ((), ()))
    nt = (((1,), (1,)), ((), ()))
    tn = (((0,), (0,)), ((), ()))
    for b in range(4):
        rows = pl.ds(NB * b, NB)
        wait_parts(min(b, 2), range(2 * (b // 3), 2 + 2 * (b // 3)))
        solved = product(rraw[rows, pl.ds(0, NB)], inverse, nt)
        newcol[rows, :] = solved
        rounded = solved.astype(BF16)
        if b == 0:
            rounded = jnp.where(row == 0, jnp.zeros_like(rounded), rounded)
        w0row[rows, :] = rounded
        r1h[rows, :], r1l[rows, :] = pair(
            rraw[rows, pl.ds(NB, NB)] - jnp.dot(rounded, w10[...], preferred_element_type=F32)
        )
    wait_parts(3, range(4))
    wait_parts(5, range(4))
    for b in range(4):
        rows = pl.ds(NB * b, NB)
        solved = product(inverse, craw[0, own, rows], nn)
        rounded = solved.astype(BF16)
        if b == 0:
            rounded = jnp.where(col == 0, jnp.zeros_like(rounded), rounded)
        w0col[:, rows] = rounded
        c1h[:, rows], c1l[:, rows] = pair(
            craw[1, own, rows] - lax.dot_general(w10[...], rounded, tn, preferred_element_type=F32)
        )

    def drain_pieces(some):
        for p in some:
            for e, on in edges_of(p):
                @pl.when(on)
                def _():
                    l_copy(p, e).wait_send()

    for u in range(7):
        for e, on in enumerate(t_on[u]):
            @pl.when(on)
            def _():
                t_copy(u, None, e).wait_send()

    @pl.when(second)
    def _():
        for u in for_first:
            for i in range(PARTS[u][2] // 4):
                s_copy(u, i).wait_send()

    for i in range(4):
        @pl.when(halves[i] & first)
        def _():
            h_copy(i).wait_send()

    @pl.when(beside)
    def _():
        a01_copy().wait_send()

    @pl.when(below)
    def _():
        a11_copy().wait_send()

    drain_pieces(range(EARLY))

    @pl.when(first & (y != 0))
    def _():
        pass_pieces(range(EARLY, PIECES))

    @pl.when(second)
    def _():
        wait_pieces(range(EARLY, PIECES))

    inverse = pair(linv[1])
    for b in range(4):
        rows = pl.ds(NB * b, NB)
        solved = product((r1h[rows, :], r1l[rows, :]), inverse, nt)
        rounded = solved.astype(BF16)
        if b == 0:
            rounded = jnp.where(row <= 1, jnp.zeros_like(rounded), rounded)
            solved = jnp.where(row == 0, rraw[rows, pl.ds(NB, NB)], solved)
        w1row[rows, :] = rounded

        @pl.when(col == 1)
        def _():
            newcol[rows, :] = solved

        solved = product(inverse, (c1h[:, rows], c1l[:, rows]), nn)
        rounded = solved.astype(BF16)
        if b == 0:
            rounded = jnp.where(col <= 1, jnp.zeros_like(rounded), rounded)
        w1col[:, rows] = rounded

    @pl.when(corner)
    def _():
        newcol[pl.ds(0, NB), :] = jnp.where(upper, 0.0, g0[:, :NB].T)

    @pl.when(below)
    def _():
        low1_copy().wait_recv()
        newcol[pl.ds(0, NB), :] = jnp.where(upper, 0.0, low1[...].T)

    drain_pieces(range(EARLY, PIECES))

    @pl.when(corner)
    def _():
        low1_copy().wait_send()


def trailing_kernel(a_ref, w0row, w1row, w0col, w1col, newcol, o_ref):
    count = o_ref.shape[0]
    rows = pl.ds(pl.multiple_of(pl.program_id(0) * count, count), count)
    update = jnp.dot(w0row[rows, :], w0col[...], preferred_element_type=F32)
    update += jnp.dot(w1row[rows, :], w1col[...], preferred_element_type=F32)
    o_ref[...] = a_ref[rows] - update.reshape(count, 8, 128)

    @pl.when(lax.axis_index("col") <= 1)
    def _():
        for t in range(2):
            o_ref[:, t, :] = newcol[rows, pl.ds(128 * t, 128)]


def on_device(covariance):
    shape = covariance.shape
    a = covariance.reshape(1024, 8, 128)
    vmem = pl.BlockSpec(memory_space=pltpu.VMEM)
    dma = pltpu.SemaphoreType.DMA
    panels = pl.pallas_call(
        gather_kernel,
        out_shape=(
            jax.ShapeDtypeStruct((1024, NB), BF16),
            jax.ShapeDtypeStruct((1024, NB), BF16),
            jax.ShapeDtypeStruct((NB, 1024), BF16),
            jax.ShapeDtypeStruct((NB, 1024), BF16),
            jax.ShapeDtypeStruct((1024, NB), F32),
        ),
        in_specs=[pl.BlockSpec(memory_space=pl.ANY)],
        out_specs=(vmem,) * 5,
        scratch_shapes=[
            pltpu.VMEM((1024, NB), F32),
            pltpu.VMEM((NB, 1024), F32),
            pltpu.VMEM((1024, 2 * NB), F32),
            pltpu.VMEM((2, 2 * NB, 1024), F32),
            pltpu.VMEM((2, NB, NB), F32),
            pltpu.VMEM((NB, NB), BF16),
            pltpu.VMEM((NB, NB), F32),
            pltpu.VMEM((NB, NB), F32),
            pltpu.VMEM((NB, NB), F32),
            pltpu.VMEM((NB, 3 * NB), F32),
            pltpu.VMEM((NB, 2 * NB), F32),
            pltpu.VMEM((8, 8, 128), F32),
            pltpu.VMEM((1024, NB), BF16),
            pltpu.VMEM((1024, NB), BF16),
            pltpu.VMEM((NB, 1024), BF16),
            pltpu.VMEM((NB, 1024), BF16),
            dma((10,)),
            dma((2, 4)),
            dma((7, 4)),
            dma((7, 16)),
            dma((7, 4)),
            dma((7, 4)),
            dma((PIECES, 14)),
            dma((PIECES,)),
            dma((3,)),
            dma((3,)),
        ],
        compiler_params=pltpu.CompilerParams(
            collective_id=0, has_side_effects=True, vmem_limit_bytes=48 << 20
        ),
        name="panels",
    )(a)
    steps = 2
    rows = 1024 // steps
    out = pl.pallas_call(
        trailing_kernel,
        grid=(steps,),
        out_shape=jax.ShapeDtypeStruct((1024, 8, 128), F32),
        in_specs=[vmem] * 6,
        out_specs=pl.BlockSpec((rows, 8, 128), lambda i: (i, 0, 0)),
        compiler_params=pltpu.CompilerParams(vmem_limit_bytes=40 << 20),
        name="trailing",
    )(a, *panels)
    return out.reshape(shape)


def solution(mesh):
    spec = P(None, "row", None, None, "col", None)
    return jax.shard_map(
        on_device, mesh=mesh, in_specs=(spec,), out_specs=spec, check_vma=False
    )
```

```python
import jax
import jax.numpy as jnp
from jax import lax
from jax.experimental import pallas as pl
from jax.experimental.pallas import tpu as pltpu
from jax.sharding import PartitionSpec as P

MESH = pl.DeviceIdType.MESH
HI = lax.Precision.HIGHEST
F32 = jnp.float32
BF16 = jnp.bfloat16
NB = 256
R_PARTS = [(32, 0, 8, 0), (32, 256, 8, 0), (32, 512, 16, 8)]
C_PARTS = [(16, 0, 16, 0), (16, 256, 16, 0)]
PARTS = R_PARTS + C_PARTS + C_PARTS
HOP = 3
EARLY = 5
PIECES = 8


def pair(value):
    high = value.astype(BF16)
    return high, (value - high.astype(F32)).astype(BF16)


def product(a, b, dims):
    (high_a, low_a), (high_b, low_b) = [v if isinstance(v, tuple) else pair(v) for v in (a, b)]

    def dot(p, q):
        return lax.dot_general(p, q, dims, preferred_element_type=F32)

    return dot(high_a, high_b) + (dot(high_a, low_b) + dot(low_a, high_b))


def lane_pick(value, lane):
    return jnp.take_along_axis(value, jnp.full(value.shape, lane, jnp.int32), axis=1)


def small_inverse(v_ref, half):
    group = lax.broadcasted_iota(jnp.int32, (8, 8, 128), 0)
    sub = lax.broadcasted_iota(jnp.int32, (8, 128), 0)

    def panel(p, _):
        r = v_ref[p]
        base = 8 * p + half
        s, low, t, inv = {}, {}, {}, []
        for k in range(8):
            c = lane_pick(r, base + k)
            for i in range(k, 8):
                s[i, k] = jnp.broadcast_to(c[i : i + 1], (8, 128))
        for k in range(8):
            rk = lax.rsqrt(s[k, k])
            inv.append(rk)
            for i in range(k + 1, 8):
                low[i, k] = s[i, k] * rk
            for j in range(k + 1, 8):
                for i in range(j, 8):
                    s[i, j] = s[i, j] - low[i, k] * low[j, k]
        for i in range(8):
            t[i, i] = inv[i]
            for j in range(i):
                acc = low[i, j] * t[j, j]
                for m in range(j + 1, i):
                    acc = acc + low[i, m] * t[m, j]
                t[i, j] = -(inv[i] * acc)
        rows = [jnp.broadcast_to(r[j : j + 1], (8, 128)) for j in range(8)]
        new = []
        for k in range(8):
            acc = t[k, 0] * rows[0]
            for j in range(1, k + 1):
                acc = acc + t[k, j] * rows[j]
            new.append(acc)
        out = new[0]
        for k in range(1, 8):
            out = jnp.where(sub == k, new[k], out)
        update = None
        for j in range(8):
            z = t[7, j] * new[7]
            for k in range(j, 7):
                z = z + t[k, j] * new[k]
            c = jnp.stack([lane_pick(v_ref[g], base + j) for g in range(8)])
            term = c * z[None]
            update = term if update is None else update + term
        v = v_ref[...]
        v_ref[...] = jnp.where(group > p, v - update, jnp.where(group == p, out[None], v))
        return 0

    lax.fori_loop(0, 8, panel, 0)


def invert_block(g_ref, v_ref, q):
    lane = lax.broadcasted_iota(jnp.int32, (64, 128), 1)
    row = lax.broadcasted_iota(jnp.int32, (64, 128), 0)
    half = (q % 2) * 64
    rows = pl.ds(pl.multiple_of(64 * q, 64), 64)
    tile = pl.ds(pl.multiple_of((q // 2) * 128, 128), 128)
    mine = (lane >= half) & (lane < half + 64)
    eye = ((lane - (64 - half)) == row).astype(F32)
    v_ref[...] = jnp.where(mine, g_ref[rows, tile], eye).reshape(8, 8, 128)
    small_inverse(v_ref, half)


def factor(g_ref, v_ref, ready, after):
    lane = lax.broadcasted_iota(jnp.int32, (64, 128), 1)
    lanes = lax.broadcasted_iota(jnp.int32, (64, NB), 1)

    def block(q, _):
        half = lax.rem(q, 2) * 64
        rows = pl.ds(pl.multiple_of(64 * q, 64), 64)
        mine = (lane >= half) & (lane < half + 64)

        @pl.when(q > 0)
        def _():
            invert_block(g_ref, v_ref, q)

        ready(q)
        t = jnp.where(mine, 0.0, v_ref[...].reshape(64, 128))
        gq = g_ref[rows, :]
        u = product(t, jnp.concatenate([gq, gq], axis=0), (((1,), (0,)), ((), ())))
        g_ref[rows, :] = u
        after(q, rows, u)
        left = jnp.where(lanes >= 64 * (q + 1), u[:, :NB], 0.0)

        @pl.when(q < 3)
        def _():
            g_ref[...] -= product(left, u, (((0,), (0,)), ((), ())))

        return 0

    lax.fori_loop(0, 4, block, 0)


def every(*conditions):
    result = conditions[0]
    for condition in conditions[1:]:
        result = result & condition
    return result


def gather_kernel(
    a_ref, w0row, w1row, w0col, w1col, newcol,
    hand_r, hand_c, rraw, craw, linv, w10, low1, a01, a11, g0, g1, v_ref, r1h, r1l, c1h, c1l,
    load_sem, h_sem, t_send, t_recv, s_send, s_recv, l_send, l_recv, x_send, x_recv,
):
    row, col = lax.axis_index("row"), lax.axis_index("col")
    x, y, z, k = row // 4, row % 4, col // 2, col % 2

    def device(x, y, z, k):
        return ((x + 4) % 4 * 4 + (y + 4) % 4, (z + 8) % 8 * 2 + (k + 2) % 2)

    def shifted(offset, sign=1):
        dx, dy, dz, dk = offset
        return (
            (x + sign * dx + 4) % 4, (y + sign * dy + 4) % 4,
            (z + sign * dz + 8) % 8, (k + sign * dk + 2) % 2,
        )

    from0 = jnp.where(y == 2, 2, jnp.where(y == 0, 0, 1))
    from1 = jnp.where(y == 3, 2, jnp.where(y == 1, 0, 1))
    back = (4 - x) % 4
    trees = [
        ([((0, 0, 1, 0), lambda x, y, z, k: (k == 1) & (z != 7))], z),
        ([((0, 0, -1, 0), lambda x, y, z, k: (k == 1) & (z != 1))], (8 - z) % 8),
        (
            [
                ((0, 0, 1, 0), lambda x, y, z, k: (k == 1) & (z <= 3)),
                ((0, 0, -1, 0), lambda x, y, z, k: (k == 1) & ((z == 0) | (z >= 6))),
            ],
            jnp.where(z > 4, 8 - z, z),
        ),
        (
            [
                ((-1, 0, 0, 0), lambda x, y, z, k: (k == 1) & (y == 0) & (x != 1)),
                ((0, 1, 0, 0), lambda x, y, z, k: (k == 1) & (y == 0) & (x != 0)),
                ((0, -1, 0, 0), lambda x, y, z, k: (k == 1) & ((y == 0) | (y == 3)) & (x != 0)),
                ((1, 0, 0, 0), lambda x, y, z, k: (k == 1) & (x == 3) & (y != 0)),
            ],
            jnp.where((x == 0) & (y != 0), 2 + from0, back + from0),
        ),
        (
            [
                ((-1, 0, 0, 0), lambda x, y, z, k: (k == 1) & (y != 0) & (x != 1)),
                ((0, 1, 0, 0), lambda x, y, z, k: (k == 1) & jnp.where(x == 0, y == 0, y == 3)),
                ((0, -1, 0, 0), lambda x, y, z, k: (k == 1) & ((y == 0) | (y == 3)) & (x == 0)),
            ],
            jnp.where((x != 0) & (y == 0), 2 + back, back + from0),
        ),
        (
            [
                ((1, 0, 0, 0), lambda x, y, z, k: (k == 1) & (y == 1) & (x != 3)),
                ((0, -1, 0, 0), lambda x, y, z, k: (k == 1) & (y == 1) & (x != 0)),
                ((0, 1, 0, 0), lambda x, y, z, k: (k == 1) & ((y == 1) | (y == 2)) & (x != 0)),
                ((-1, 0, 0, 0), lambda x, y, z, k: (k == 1) & (x == 1) & (y != 1)),
            ],
            jnp.where((x == 0) & (y != 1), 2 + from1, x + from1),
        ),
        (
            [
                ((1, 0, 0, 0), lambda x, y, z, k: (k == 1) & (y != 1) & (x != 3)),
                ((0, -1, 0, 0), lambda x, y, z, k: (k == 1) & jnp.where(x == 0, y == 1, y == 2)),
                ((0, 1, 0, 0), lambda x, y, z, k: (k == 1) & ((y == 1) | (y == 2)) & (x == 0)),
            ],
            jnp.where((x != 0) & (y == 1), 2 + x, x + from1),
        ),
    ]

    def branch(y, k):
        return (y == 0) & (k == 0)

    def entry(z):
        return jnp.where(z == 4, 2, jnp.where((z == 2) | (z == 6), 1, jnp.where((z == 3) | (z == 5), 3, 0)))

    def along_z(at):
        return lambda x, y, z, k: branch(y, k) & (z == 0) & (x == at)

    def along_x(x, y, z, k):
        return branch(y, k) & (x == entry(z))

    def along_y(x, y, z, k):
        return branch(y, k)

    l_edges = [
        ((1, 0, 0, 0), lambda x, y, z, k: branch(y, k) & ((x == entry(z)) | (x == (entry(z) + 1) % 4))),
        ((-1, 0, 0, 0), along_x),
        ((0, 0, 1, 0), along_z(0)),
        ((0, 0, -1, 0), along_z(0)),
        ((0, 0, 2, 0), along_z(1)),
        ((0, 0, -2, 0), along_z(1)),
        ((0, 0, 4, 0), along_z(2)),
        ((0, 0, 3, 0), along_z(3)),
        ((0, 0, -3, 0), along_z(3)),
        ((0, -1, 0, 0), lambda x, y, z, k: (y == 3) & (k == 0)),
        ((0, 2, 0, 0), along_y),
        ((0, 1, 0, 0), along_y),
        ((0, -1, 0, 0), along_y),
        ((0, 0, 0, 1), lambda x, y, z, k: k == 0),
    ]
    early_edge, late_edge = 9, 10
    corner = every(row == 0, col == 0)
    beside = every(row == 0, col == 1)
    below = every(row == 1, col == 1)
    first, second = k == 0, k == 1
    r_source = z == 0
    c_source = [every(x == 0, y == 0), every(x == 0, y == 1)]
    root = [r_source, r_source, r_source, c_source[0], c_source[0], c_source[1], c_source[1]]

    def r_load(t, dst, lane):
        return pltpu.make_async_copy(
            a_ref.at[:, t, :], dst.at[:, pl.ds(lane + 128 * t, 128)], load_sem.at[t]
        )

    def c_load(t, dst):
        return pltpu.make_async_copy(
            a_ref.at[pl.ds(0, NB), t, :], dst.at[:, pl.ds(128 * t, 128)], load_sem.at[2 + t]
        )

    own = pl.ds(pl.multiple_of(NB * k, NB), NB)

    def c_loads(act, some):
        for s in range(2):
            @pl.when(c_source[s] & first)
            def _():
                for t in some:
                    act(c_load(t, hand_c))

            @pl.when(c_source[s] & second)
            def _():
                for t in some:
                    act(c_load(t, craw.at[s, pl.ds(NB, NB)]))

    def r_loads(act):
        @pl.when(r_source)
        def _():
            for t in range(2):
                act(r_load(t, hand_r, 0))

    c_loads(lambda copy: copy.start(), range(8))
    r_loads(lambda copy: copy.start())

    barrier = pltpu.get_barrier_semaphore()

    def greet(target):
        pl.semaphore_signal(barrier, inc=1, device_id=device(*target), device_id_type=MESH)

    awaited = jnp.where(beside, 2, 1) + jnp.where(below, 1, 0) + jnp.where(corner, 1, 0)
    greet((x, y, z, 1 - k))
    for offset, sends in [edge for edges, _ in trees for edge in edges] + l_edges[:-1]:
        awaited = awaited + sends(x, y, z, k).astype(jnp.int32)
        parent = shifted(offset, -1)

        @pl.when(sends(*parent))
        def _():
            greet(parent)

    @pl.when(corner)
    def _():
        greet((0, 0, 0, 1))
        greet((0, 1, 0, 1))

    @pl.when(below)
    def _():
        greet((0, 0, 0, 0))

    linv[0, pl.ds(0, 128), pl.ds(128, 128)] = jnp.zeros((128, 128), F32)
    linv[1, pl.ds(0, 128), pl.ds(128, 128)] = jnp.zeros((128, 128), F32)
    c_loads(lambda copy: copy.wait(), range(2))

    @pl.when(corner)
    def _():
        eye = (
            lax.broadcasted_iota(jnp.int32, (NB, NB), 0) == lax.broadcasted_iota(jnp.int32, (NB, NB), 1)
        ).astype(F32)
        g0[:, :NB] = hand_c[:, :NB]
        g0[:, 2 * NB :] = eye
        g1[:, :NB] = jnp.zeros((NB, NB), F32)
        g1[:, NB:] = eye
        invert_block(g0, v_ref, 0)

    pl.semaphore_wait(barrier, awaited)

    def remote(src, dst, send, recv, target):
        return pltpu.make_async_remote_copy(
            src_ref=src, dst_ref=dst, send_sem=send, recv_sem=recv,
            device_id=target, device_id_type=MESH,
        )

    t_on = [[sends(x, y, z, k) for _, sends in edges] for edges, _ in trees]
    t_to = [[device(*shifted(offset)) for offset, _ in edges] for edges, _ in trees]
    l_on = [sends(x, y, z, k) for _, sends in l_edges]
    l_to = [device(*shifted(offset)) for offset, _ in l_edges]
    sibling = device(x, y, z, 1 - k)
    first_step = [PARTS[u][3] + HOP * depth for u, (_, depth) in enumerate(trees)]

    def t_ref(u, start, count):
        rows, top, _, _ = PARTS[u]
        span = pl.ds(pl.multiple_of(top + rows * start, rows), rows * count)
        return rraw.at[span, :] if u < 3 else craw.at[(u - 3) // 2, span, :]

    def t_copy(u, n, e=0):
        part = t_ref(u, 0, PARTS[u][2]) if n is None else t_ref(u, n, 1)
        return remote(part, part, t_send.at[u, e], t_recv.at[u, 0 if n is None else n], t_to[u][e])

    def s_copy(u, i):
        part = t_ref(u, 4 * i, 4)
        return remote(part, part, s_send.at[u, i], s_recv.at[u, i], sibling)

    for_first = (0, 1, 2, 3, 5)

    def h_copy(i):
        if i < 2:
            src, dst = hand_r.at[pl.ds(512 * i, 512), :], rraw.at[pl.ds(512 * i, 512), pl.ds(0, NB)]
        else:
            half = pl.ds(128 * (i - 2), 128)
            src, dst = hand_c.at[half, :], craw.at[row % 2, half, :]
        return remote(src, dst, h_sem.at[0, i], h_sem.at[1, i], sibling)

    pieces = [
        linv.at[0, pl.ds(0, 128), pl.ds(0, 128)],
        w10.at[pl.ds(0, 128), :],
        linv.at[0, pl.ds(128, 64), :],
        linv.at[0, pl.ds(192, 64), :],
        w10.at[pl.ds(128, 128), :],
        linv.at[1, pl.ds(0, 128), pl.ds(0, 128)],
        linv.at[1, pl.ds(128, 64), :],
        linv.at[1, pl.ds(192, 64), :],
    ]

    def l_copy(p, e):
        return remote(pieces[p], pieces[p], l_send.at[p, e], l_recv.at[p], l_to[e])

    def edges_of(p):
        skipped = late_edge if p < EARLY else early_edge
        return [(e, on) for e, on in enumerate(l_on) if e != skipped]

    def send_piece(p):
        for e, on in edges_of(p):
            @pl.when(on)
            def _():
                l_copy(p, e).start()

    def wait_pieces(some):
        for p in some:
            l_copy(p, 0).wait_recv()

    def pass_pieces(some):
        for p in some:
            l_copy(p, 0).wait_recv()
            send_piece(p)

    def a01_copy():
        return remote(craw.at[0, pl.ds(NB, NB), pl.ds(0, NB)], a01, x_send.at[0], x_recv.at[0], (0, 0))

    def a11_copy():
        return remote(craw.at[1, pl.ds(NB, NB), pl.ds(0, NB)], a11, x_send.at[1], x_recv.at[1], (0, 0))

    def low1_copy():
        return remote(low1, low1, x_send.at[2], x_recv.at[2], (1, 1))

    @pl.when(beside)
    def _():
        a01_copy().start()

    @pl.when(below)
    def _():
        a11_copy().start()

    c_root = c_source[0] | c_source[1]
    halves = [r_source, r_source, c_root, c_root]

    def hand_over():
        c_loads(lambda copy: copy.wait(), range(2, 8))
        r_loads(lambda copy: copy.wait())
        for i in (0, 2, 1, 3):
            @pl.when(halves[i] & first)
            def _():
                h_copy(i).start()

    hand_over()

    @pl.when(r_source & second)
    def _():
        rraw[:, NB:] = hand_r[...]

    @pl.when(corner)
    def _():
        def ready0(q):
            @pl.when(q == 0)
            def _():
                a01_copy().wait_recv()
                g0[:, NB : 2 * NB] = a01[...]

        def after0(q, rows, u):
            linv[0, rows, :] = u[:, 2 * NB :]
            w = u[:, NB : 2 * NB].astype(BF16)
            w10[rows, :] = w
            g1[:, :NB] -= lax.dot_general(w, w, (((0,), (0,)), ((), ())), preferred_element_type=F32)

            @pl.when(q == 1)
            def _():
                send_piece(0)
                send_piece(1)

            @pl.when(q == 2)
            def _():
                send_piece(2)

            @pl.when(q == 3)
            def _():
                send_piece(3)
                send_piece(4)

        factor(g0, v_ref, ready0, after0)
        a11_copy().wait_recv()
        g1[:, :NB] += a11[...]
        invert_block(g1, v_ref, 0)

        def after1(q, rows, u):
            linv[1, rows, :] = u[:, NB:]
            low1[rows, :] = u[:, :NB]
            for i in range(3):
                @pl.when(q == i + 1)
                def _():
                    send_piece(EARLY + i)

        factor(g1, v_ref, lambda q: None, after1)
        low1_copy().start()

    @pl.when(first & jnp.logical_not(corner))
    def _():
        pass_pieces(range(EARLY))

    @pl.when(branch(y, k) & jnp.logical_not(corner))
    def _():
        pass_pieces(range(EARLY, PIECES))

    @pl.when(second)
    def _():
        def step(m, _):
            for i in range(4):
                @pl.when(halves[i] & (m == 8 * (i % 2)))
                def _():
                    h_copy(i).wait_recv()

            for u in range(7):
                n = m - first_step[u]

                @pl.when((n >= 0) & (n < PARTS[u][2]))
                def _():
                    @pl.when(jnp.logical_not(root[u]))
                    def _():
                        t_copy(u, n).wait_recv()

                    for e, on in enumerate(t_on[u]):
                        @pl.when(on)
                        def _():
                            t_copy(u, n, e).start()

                    if u in for_first:
                        @pl.when(n % 4 == 3)
                        def _():
                            s_copy(u, n // 4).start()

            return 0

        lax.fori_loop(0, 40, step, 0)
        wait_pieces(range(EARLY))

    def wait_parts(u, some):
        @pl.when(first)
        def _():
            for i in some:
                s_copy(u, i).wait_recv()

    inverse = pair(linv[0])
    upper = lax.broadcasted_iota(jnp.int32, (NB, NB), 1) > lax.broadcasted_iota(jnp.int32, (NB, NB), 0)
    nn = (((1,), (0,)), ((), ()))
    nt = (((1,), (1,)), ((), ()))
    tn = (((0,), (0,)), ((), ()))
    for b in range(4):
        rows = pl.ds(NB * b, NB)
        wait_parts(min(b, 2), range(2 * (b // 3), 2 + 2 * (b // 3)))
        solved = product(rraw[rows, pl.ds(0, NB)], inverse, nt)
        newcol[rows, :] = solved
        rounded = solved.astype(BF16)
        if b == 0:
            rounded = jnp.where(row == 0, jnp.zeros_like(rounded), rounded)
        w0row[rows, :] = rounded
        r1h[rows, :], r1l[rows, :] = pair(
            rraw[rows, pl.ds(NB, NB)] - jnp.dot(rounded, w10[...], preferred_element_type=F32)
        )
    wait_parts(3, range(4))
    wait_parts(5, range(4))
    for b in range(4):
        rows = pl.ds(NB * b, NB)
        solved = product(inverse, craw[0, own, rows], nn)
        rounded = solved.astype(BF16)
        if b == 0:
            rounded = jnp.where(col == 0, jnp.zeros_like(rounded), rounded)
        w0col[:, rows] = rounded
        c1h[:, rows], c1l[:, rows] = pair(
            craw[1, own, rows] - lax.dot_general(w10[...], rounded, tn, preferred_element_type=F32)
        )

    def drain_pieces(some):
        for p in some:
            for e, on in edges_of(p):
                @pl.when(on)
                def _():
                    l_copy(p, e).wait_send()

    for u in range(7):
        for e, on in enumerate(t_on[u]):
            @pl.when(on)
            def _():
                t_copy(u, None, e).wait_send()

    @pl.when(second)
    def _():
        for u in for_first:
            for i in range(PARTS[u][2] // 4):
                s_copy(u, i).wait_send()

    for i in range(4):
        @pl.when(halves[i] & first)
        def _():
            h_copy(i).wait_send()

    @pl.when(beside)
    def _():
        a01_copy().wait_send()

    @pl.when(below)
    def _():
        a11_copy().wait_send()

    drain_pieces(range(EARLY))

    @pl.when(first & (y != 0))
    def _():
        pass_pieces(range(EARLY, PIECES))

    @pl.when(second)
    def _():
        wait_pieces(range(EARLY, PIECES))

    inverse = pair(linv[1])
    for b in range(4):
        rows = pl.ds(NB * b, NB)
        solved = product((r1h[rows, :], r1l[rows, :]), inverse, nt)
        rounded = solved.astype(BF16)
        if b == 0:
            rounded = jnp.where(row <= 1, jnp.zeros_like(rounded), rounded)
            solved = jnp.where(row == 0, rraw[rows, pl.ds(NB, NB)], solved)
        w1row[rows, :] = rounded

        @pl.when(col == 1)
        def _():
            newcol[rows, :] = solved

        solved = product(inverse, (c1h[:, rows], c1l[:, rows]), nn)
        rounded = solved.astype(BF16)
        if b == 0:
            rounded = jnp.where(col <= 1, jnp.zeros_like(rounded), rounded)
        w1col[:, rows] = rounded

    @pl.when(corner)
    def _():
        newcol[pl.ds(0, NB), :] = jnp.where(upper, 0.0, g0[:, :NB].T)

    @pl.when(below)
    def _():
        low1_copy().wait_recv()
        newcol[pl.ds(0, NB), :] = jnp.where(upper, 0.0, low1[...].T)

    drain_pieces(range(EARLY, PIECES))

    @pl.when(corner)
    def _():
        low1_copy().wait_send()


def trailing_kernel(a_ref, w0row, w1row, w0col, w1col, newcol, o_ref):
    count = o_ref.shape[0]
    rows = pl.ds(pl.multiple_of(pl.program_id(0) * count, count), count)
    update = jnp.dot(w0row[rows, :], w0col[...], preferred_element_type=F32)
    update += jnp.dot(w1row[rows, :], w1col[...], preferred_element_type=F32)
    o_ref[...] = a_ref[rows] - update.reshape(count, 8, 128)

    @pl.when(lax.axis_index("col") <= 1)
    def _():
        for t in range(2):
            o_ref[:, t, :] = newcol[rows, pl.ds(128 * t, 128)]


def on_device(covariance):
    shape = covariance.shape
    a = covariance.reshape(1024, 8, 128)
    vmem = pl.BlockSpec(memory_space=pltpu.VMEM)
    dma = pltpu.SemaphoreType.DMA
    panels = pl.pallas_call(
        gather_kernel,
        out_shape=(
            jax.ShapeDtypeStruct((1024, NB), BF16),
            jax.ShapeDtypeStruct((1024, NB), BF16),
            jax.ShapeDtypeStruct((NB, 1024), BF16),
            jax.ShapeDtypeStruct((NB, 1024), BF16),
            jax.ShapeDtypeStruct((1024, NB), F32),
        ),
        in_specs=[pl.BlockSpec(memory_space=pl.ANY)],
        out_specs=(vmem,) * 5,
        scratch_shapes=[
            pltpu.VMEM((1024, NB), F32),
            pltpu.VMEM((NB, 1024), F32),
            pltpu.VMEM((1024, 2 * NB), F32),
            pltpu.VMEM((2, 2 * NB, 1024), F32),
            pltpu.VMEM((2, NB, NB), F32),
            pltpu.VMEM((NB, NB), BF16),
            pltpu.VMEM((NB, NB), F32),
            pltpu.VMEM((NB, NB), F32),
            pltpu.VMEM((NB, NB), F32),
            pltpu.VMEM((NB, 3 * NB), F32),
            pltpu.VMEM((NB, 2 * NB), F32),
            pltpu.VMEM((8, 8, 128), F32),
            pltpu.VMEM((1024, NB), BF16),
            pltpu.VMEM((1024, NB), BF16),
            pltpu.VMEM((NB, 1024), BF16),
            pltpu.VMEM((NB, 1024), BF16),
            dma((10,)),
            dma((2, 4)),
            dma((7, 4)),
            dma((7, 16)),
            dma((7, 4)),
            dma((7, 4)),
            dma((PIECES, 14)),
            dma((PIECES,)),
            dma((3,)),
            dma((3,)),
        ],
        compiler_params=pltpu.CompilerParams(
            collective_id=0, has_side_effects=True, vmem_limit_bytes=48 << 20
        ),
        name="panels",
    )(a)
    steps = 2
    rows = 1024 // steps
    out = pl.pallas_call(
        trailing_kernel,
        grid=(steps,),
        out_shape=jax.ShapeDtypeStruct((1024, 8, 128), F32),
        in_specs=[vmem] * 6,
        out_specs=pl.BlockSpec((rows, 8, 128), lambda i: (i, 0, 0)),
        compiler_params=pltpu.CompilerParams(vmem_limit_bytes=40 << 20),
        name="trailing",
    )(a, *panels)
    return out.reshape(shape)


def solution(mesh):
    spec = P(None, "row", None, None, "col", None)
    return jax.shard_map(
        on_device, mesh=mesh, in_specs=(spec,), out_specs=spec, check_vma=False
    )
```
